32 devices in a mesh: dp: 8 (over z, x), ctx: 4 (over y, core).
Axes of the slice: x: 2, y: 2, z: 4, core: 2. Of those that a mesh axis runs over, the one named last changes fastest.
Arguments:
- prefix_tokens: bfloat16 [8, 624, 2048], P('dp', 'ctx'), may hold values from -6 to 6
- actions: bfloat16 [8, 4, 50, 32], P('dp', 'ctx'), may hold values from -6 to 6
- robot_state: bfloat16 [8, 32], P('dp'), may hold values from -6 to 6
- text_len: int32 [8], P('dp'), may hold values from 5 to 48, as said below
- flow_index: int32 [8, 4], P('dp', 'ctx'), may hold values from 0 to 999
- query_pre: bfloat16 [2048, 2048], P(('dp', 'ctx')), may hold values from -0.125 to 0.125
- key_pre: bfloat16 [2048, 256], P(('dp', 'ctx')), may hold values from -0.125 to 0.125
- value_pre: bfloat16 [2048, 256], P(('dp', 'ctx')), may hold values from -0.125 to 0.125
- out_pre: bfloat16 [2048, 2048], P(('dp', 'ctx')), may hold values from -1.5 to 1.5
- gain_attn_pre: bfloat16 [2048], P(('dp', 'ctx')), may hold values from 0.5 to 1.5
- gain_ffn_pre: bfloat16 [2048], P(('dp', 'ctx')), may hold values from 0.5 to 1.5
- query_act: bfloat16 [1024, 2048], P(('dp', 'ctx')), may hold values from -0.1875 to 0.1875
- key_act: bfloat16 [1024, 256], P(('dp', 'ctx')), may hold values from -0.1875 to 0.1875
- value_act: bfloat16 [1024, 256], P(('dp', 'ctx')), may hold values from -0.1875 to 0.1875
- out_act: bfloat16 [2048, 1024], P(('dp', 'ctx')), may hold values from -1.5 to 1.5
- gain_attn_act: bfloat16 [1024], P(('dp', 'ctx')), may hold values from 0.5 to 1.5
- gain_ffn_act: bfloat16 [1024], P(('dp', 'ctx')), may hold values from 0.5 to 1.5
- action_in: bfloat16 [1024, 32], P(('dp', 'ctx')), may hold values from -1 to 1
- mix_first: bfloat16 [2048, 1024], P(('dp', 'ctx')), may hold values from -0.125 to 0.125
- mix_second: bfloat16 [1024, 1024], P(('dp', 'ctx')), may hold values from -0.1875 to 0.1875
- state_in: bfloat16 [1024, 32], P(('dp', 'ctx')), may hold values from -1 to 1
- gate_pre: bfloat16 [2048, 16384], P('dp', 'ctx'), may hold values from -0.125 to 0.125
- up_pre: bfloat16 [2048, 16384], P('dp', 'ctx'), may hold values from -0.125 to 0.125
- down_pre: bfloat16 [16384, 2048], P('ctx', 'dp'), may hold values from -0.046875 to 0.046875
- gate_act: bfloat16 [1024, 4096], P('dp', 'ctx'), may hold values from -0.1875 to 0.1875
- up_act: bfloat16 [1024, 4096], P('dp', 'ctx'), may hold values from -0.1875 to 0.1875
- down_act: bfloat16 [4096, 1024], P('ctx', 'dp'), may hold values from -0.09375 to 0.09375
- grad_pre: bfloat16 [8, 624, 2048], P('dp', 'ctx'), may hold values from -6 to 6
- grad_act: bfloat16 [8, 4, 51, 1024], P('dp', 'ctx'), may hold values from -6 to 6
Outputs:
- out_prefix: float32 [8, 624, 2048], P('dp', 'ctx')
- out_actions: float32 [8, 4, 51, 1024], P('dp', 'ctx')
- grad_prefix: float32 [8, 624, 2048], P('dp', 'ctx')
- grad_actions: float32 [8, 4, 50, 32], P('dp', 'ctx')
- grad_query_pre: float32 [2048, 2048], P(('dp', 'ctx'))
- grad_key_pre: float32 [2048, 256], P(('dp', 'ctx'))
- grad_value_pre: float32 [2048, 256], P(('dp', 'ctx'))
- grad_out_pre: float32 [2048, 2048], P(('dp', 'ctx'))
- grad_gain_attn_pre: float32 [2048], P(('dp', 'ctx'))
- grad_gain_ffn_pre: float32 [2048], P(('dp', 'ctx'))
- grad_query_act: float32 [1024, 2048], P(('dp', 'ctx'))
- grad_key_act: float32 [1024, 256], P(('dp', 'ctx'))
- grad_value_act: float32 [1024, 256], P(('dp', 'ctx'))
- grad_out_act: float32 [2048, 1024], P(('dp', 'ctx'))
- grad_gain_attn_act: float32 [1024], P(('dp', 'ctx'))
- grad_gain_ffn_act: float32 [1024], P(('dp', 'ctx'))
- grad_action_in: float32 [1024, 32], P(('dp', 'ctx'))
- grad_mix_first: float32 [2048, 1024], P(('dp', 'ctx'))
- grad_mix_second: float32 [1024, 1024], P(('dp', 'ctx'))
- grad_state_in: float32 [1024, 32], P(('dp', 'ctx'))
- grad_gate_pre: float32 [2048, 16384], P('dp', 'ctx')
- grad_up_pre: float32 [2048, 16384], P('dp', 'ctx')
- grad_down_pre: float32 [16384, 2048], P('ctx', 'dp')
- grad_gate_act: float32 [1024, 4096], P('dp', 'ctx')
- grad_up_act: float32 [1024, 4096], P('dp', 'ctx')
- grad_down_act: float32 [4096, 1024], P('ctx', 'dp')
The draws below stay inside these ranges and needn't reach their ends.
Inputs may be any that keep to these rules, and one draw needn't show every extreme that they name: `text_len`: the rest of the 48 text slots are padding; some item has exactly 48 given tokens and another exactly 5.
All inputs are finite; a program needn't handle non-finite values.
Results may differ from the reference program's by a relative error of at most 0.024.
Values may be sent and summed in bfloat16 or wider, within the bound.
No kernel may reach another device: no remote copies, remote signals or barrier semaphores. Data moves between devices by JAX's collectives and lax.ppermute only.
A program may use at most 384 MiB of HBM per device.

```python
import math
import jax
import jax.numpy as jnp
from jax import lax

D = 2048
DS = 1024
HEADS = 8
HD = 256
FF = 16384
FFS = 4096
ACTD = 32
ACT = 50
CAMS = 3
PATCH = 192
TXT = 48
NTIME = 1000
ITEMS = 8
FLOWS = 4
PRE = 624
SUF = 51


def draw_text_len(key, part):
    key = jax.random.fold_in(key, 11)
    first_key, second_key = jax.random.split(key)
    lengths = jax.random.randint(first_key, (ITEMS,), 5, TXT + 1)
    chosen = jax.random.randint(second_key, (), 0, ITEMS)
    places = jnp.arange(ITEMS)
    lengths = jnp.where(places == chosen, TXT, lengths)
    lengths = jnp.where(places == (chosen + 1) % ITEMS, 5, lengths)
    return lengths.astype(jnp.int32)


def set_ends(drawn, key, smallest, high):
    shape = drawn.shape
    spot = [jax.random.randint(jax.random.fold_in(key, axis), (), 0, shape[axis]) for axis in range(len(shape))]
    drawn = drawn.at[tuple(spot)].set(smallest)
    longest = shape.index(max(shape))
    spot[longest] = (spot[longest] + 1) % shape[longest]
    return drawn.at[tuple(spot)].set(high)


def block_levels(key, dims, cuts, low, top_value):
    level = 1.0
    for axis_at, shards_of in cuts:
        heights = jax.random.uniform(jax.random.fold_in(jax.random.fold_in(key, 6), axis_at), (shards_of,), jnp.float32, low / len(cuts), top_value / len(cuts))
        level = level * jnp.repeat(jnp.exp(heights), dims[axis_at] // shards_of).reshape((-1,) + (1,) * (len(dims) - 1 - axis_at))
    return level


def bell_draw(own_key, dims, spread, limit, shards=(), kind=jnp.bfloat16):
    factor_of = block_levels(own_key, dims, shards, -0.22, 0.18) if shards else 1.0
    array = jax.random.normal(own_key, dims, jnp.float32) * spread * factor_of
    return jnp.minimum(jnp.maximum(array, -limit), limit).astype(kind)


def setup_inputs(seed: int = 0) -> dict:
    seeds = jax.random.split(jax.random.key(seed), 30)
    return {
        "prefix_tokens": bell_draw(seeds[0], (ITEMS, PRE, D), 1.0, 6.0, ((0, 8), (1, 4))),
        "actions": bell_draw(seeds[1], (ITEMS, FLOWS, ACT, ACTD), 1.0, 6.0, ((0, 8), (1, 4))),
        "robot_state": bell_draw(seeds[2], (ITEMS, ACTD), 1.0, 6.0, ((0, 8),)),
        "text_len": draw_text_len(jax.random.fold_in(seeds[29], 71), 0),
        "flow_index": set_ends(jax.random.randint(seeds[4], (ITEMS, FLOWS), 0, NTIME), jax.random.fold_in(seeds[4], 1), 0, NTIME - 1).astype(jnp.int32),
        "query_pre": bell_draw(seeds[5], (D, HEADS * HD), D ** -0.5, 0.125, ((0, 32),)),
        "key_pre": bell_draw(seeds[6], (D, HD), D ** -0.5, 0.125, ((0, 32),)),
        "value_pre": bell_draw(seeds[7], (D, HD), D ** -0.5, 0.125, ((0, 32),)),
        "out_pre": bell_draw(seeds[8], (HEADS * HD, D), (HD // 16) ** -0.5, 1.5, ((0, 32),)),
        "gain_attn_pre": jnp.clip(1.0 + 0.1 * jax.random.normal(seeds[9], (D,), jnp.float32), 0.5, 1.5).astype(jnp.bfloat16),
        "gain_ffn_pre": jnp.clip(1.0 + 0.1 * jax.random.normal(seeds[10], (D,), jnp.float32), 0.5, 1.5).astype(jnp.bfloat16),
        "query_act": bell_draw(seeds[11], (DS, HEADS * HD), DS ** -0.5, 0.1875, ((0, 32),)),
        "key_act": bell_draw(seeds[12], (DS, HD), DS ** -0.5, 0.1875, ((0, 32),)),
        "value_act": bell_draw(seeds[13], (DS, HD), DS ** -0.5, 0.1875, ((0, 32),)),
        "out_act": bell_draw(seeds[14], (HEADS * HD, DS), (HD // 16) ** -0.5, 1.5, ((0, 32),)),
        "gain_attn_act": jnp.clip(1.0 + 0.1 * jax.random.normal(seeds[15], (DS,), jnp.float32), 0.5, 1.5).astype(jnp.bfloat16),
        "gain_ffn_act": jnp.clip(1.0 + 0.1 * jax.random.normal(seeds[16], (DS,), jnp.float32), 0.5, 1.5).astype(jnp.bfloat16),
        "action_in": bell_draw(seeds[17], (DS, ACTD), ACTD ** -0.5, 1.0, ((0, 32),)),
        "mix_first": bell_draw(seeds[18], (2 * DS, DS), (2 * DS) ** -0.5, 0.125, ((0, 32),)),
        "mix_second": bell_draw(seeds[19], (DS, DS), DS ** -0.5, 0.1875, ((0, 32),)),
        "state_in": bell_draw(seeds[20], (DS, ACTD), ACTD ** -0.5, 1.0, ((0, 32),)),
        "gate_pre": bell_draw(seeds[21], (D, FF), D ** -0.5, 0.125, ((0, 8), (1, 4))),
        "up_pre": bell_draw(seeds[22], (D, FF), D ** -0.5, 0.125, ((0, 8), (1, 4))),
        "down_pre": bell_draw(seeds[23], (FF, D), FF ** -0.5, 0.046875, ((0, 4), (1, 8))),
        "gate_act": bell_draw(seeds[24], (DS, FFS), DS ** -0.5, 0.1875, ((0, 8), (1, 4))),
        "up_act": bell_draw(seeds[25], (DS, FFS), DS ** -0.5, 0.1875, ((0, 8), (1, 4))),
        "down_act": bell_draw(seeds[26], (FFS, DS), FFS ** -0.5, 0.09375, ((0, 4), (1, 8))),
        "grad_pre": bell_draw(seeds[27], (ITEMS, PRE, D), 1.0, 6.0, ((0, 8), (1, 4))),
        "grad_act": bell_draw(seeds[28], (ITEMS, FLOWS, SUF, DS), 1.0, 6.0, ((0, 8), (1, 4))),
    }


@jax.custom_vjp
def low(v):
    return lax.optimization_barrier(v.astype(jnp.bfloat16)).astype(jnp.float32)

@jax.custom_vjp
def low_back(v):
    return v

def low_keep(v):
    return (low(v), None)

def low_pass(kept, grad):
    return (grad,)

def back_keep(v):
    return (v, None)

def back_low(kept, grad):
    return (low(grad),)
low.defvjp(low_keep, low_pass)
low_back.defvjp(back_keep, back_low)

def matmul(left, right):
    return jnp.matmul(left, right, precision=lax.Precision.HIGHEST)

def rms_norm(values, norm_gain):
    return values * lax.rsqrt(lax.optimization_barrier(jnp.mean(values * values, axis=-1, keepdims=True)) + 1e-06) * norm_gain

def time_embed(sample_index):
    flow_time = (sample_index.astype(jnp.float32) + 0.5) / NTIME
    halves = DS // 2
    fraction = jnp.arange(halves, dtype=jnp.float32) / (halves - 1)
    period = 0.004 * jnp.power(1000.0, fraction)
    angles = 2.0 * math.pi * flow_time[..., None] / period
    return jnp.concatenate([jnp.sin(angles), jnp.cos(angles)], axis=-1)

def project(normed, weight):
    return low_back(low(matmul(normed, weight)))

def attend(queries, key_rows, value_rows, allowed):
    row_count = queries.shape[0]
    query_head_rows = queries.reshape(row_count, HEADS, HD)
    scores = jnp.einsum('qhd,kd->hqk', query_head_rows, key_rows, precision=lax.Precision.HIGHEST) * HD ** (-0.5)
    scores = low_back(scores)
    scores = jnp.where(allowed[None], scores, -1e+30)
    attn_probs = jax.nn.softmax(scores, axis=-1)
    mixture = jnp.einsum('hqk,kd->qhd', low(attn_probs), value_rows, precision=lax.Precision.HIGHEST)
    return mixture.reshape(row_count, HEADS * HD)

def feed_forward(middle, norm_gain, gate_weight, up_weight, down_weight):
    normed = low(rms_norm(middle, norm_gain))
    gate_value = low_back(matmul(normed, gate_weight))
    up_value = low_back(matmul(normed, up_weight))
    hidden = low(jax.nn.gelu(gate_value, approximate=True) * up_value)
    return middle + low_back(matmul(hidden, down_weight))

def layer_forward(weights, prefix, actions, robot_state, text_len, flow_index):
    query_pre, key_pre, value_pre, out_pre, gain_attn_pre, gain_ffn_pre, query_act, key_act, value_act, out_act, gain_attn_act, gain_ffn_act, action_in, mix_first, mix_second, state_in, gate_pre, up_pre, down_pre, gate_act, up_act, down_act = weights
    flow_count = actions.shape[0]
    time_rows = time_embed(flow_index)
    action_emb = matmul(actions, action_in.T)
    mix_input = low_back(low(jnp.concatenate([action_emb, jnp.broadcast_to(time_rows[:, None, :], action_emb.shape)], axis=-1)))
    pre_mix = low_back(matmul(mix_input, mix_first))
    action_rows = low_back(matmul(low(jax.nn.silu(pre_mix)), mix_second))
    state_rows = low_back(matmul(jnp.broadcast_to(robot_state[None, :], (flow_count, robot_state.shape[0])), state_in.T))
    side_input = jnp.concatenate([state_rows[:, None, :], action_rows], axis=1)
    normed_pre = low(rms_norm(prefix, gain_attn_pre))
    normed_act = low(rms_norm(side_input, gain_attn_act))
    queries_pre = project(normed_pre, query_pre)
    keys_pre = project(normed_pre, key_pre)
    values_pre = project(normed_pre, value_pre)
    queries_act = project(normed_act, query_act)
    keys_act = project(normed_act, key_act)
    values_act = project(normed_act, value_act)
    positions = jnp.arange(PRE)
    camera_rows = CAMS * PATCH
    key_valid = (positions < camera_rows) | (positions - camera_rows < text_len)
    attn_pre = attend(queries_pre, keys_pre, values_pre, jnp.broadcast_to(key_valid[None, :], (PRE, PRE)))
    groups = jnp.arange(SUF) > 0
    own_block = groups[None, :] <= groups[:, None]
    allowed_act = jnp.concatenate([jnp.broadcast_to(key_valid[None, :], (SUF, PRE)), own_block], axis=1)

    def flow_attend(queries, key_rows, value_rows):
        return attend(queries, jnp.concatenate([keys_pre, key_rows], axis=0), jnp.concatenate([values_pre, value_rows], axis=0), allowed_act)
    attn_act = jax.vmap(flow_attend)(queries_act, keys_act, values_act)
    mid_pre = prefix + low_back(matmul(low_back(low(attn_pre)), out_pre))
    mid_act = side_input + low_back(matmul(low_back(low(attn_act)), out_act))
    return (feed_forward(mid_pre, gain_ffn_pre, gate_pre, up_pre, down_pre), feed_forward(mid_act, gain_ffn_act, gate_act, up_act, down_act))

def reference(prefix_tokens, actions, robot_state, text_len, flow_index, query_pre, key_pre, value_pre, out_pre, gain_attn_pre, gain_ffn_pre, query_act, key_act, value_act, out_act, gain_attn_act, gain_ffn_act, action_in, mix_first, mix_second, state_in, gate_pre, up_pre, down_pre, gate_act, up_act, down_act, grad_pre, grad_act):
    weights = tuple((weight.astype(jnp.float32) for weight in (query_pre, key_pre, value_pre, out_pre, gain_attn_pre, gain_ffn_pre, query_act, key_act, value_act, out_act, gain_attn_act, gain_ffn_act, action_in, mix_first, mix_second, state_in, gate_pre, up_pre, down_pre, gate_act, up_act, down_act)))
    zero_grads = tuple((jnp.zeros(weight.shape, jnp.float32) for weight in weights))

    def one_item(running, item_data):
        prefix, item_actions, item_state, item_len, item_flow, cot_pre, cot_act = item_data
        state_float = item_state.astype(jnp.float32)

        def forward(params, prefix_in, actions_in):
            return layer_forward(params, prefix_in, actions_in, state_float, item_len, item_flow)
        outputs, pullback = jax.vjp(forward, weights, prefix.astype(jnp.float32), item_actions.astype(jnp.float32))
        weight_grads, prefix_grad, action_grad = pullback((cot_pre.astype(jnp.float32), cot_act.astype(jnp.float32)))
        running = tuple((before + increment for before, increment in zip(running, weight_grads)))
        return (running, (outputs[0], outputs[1], prefix_grad, action_grad))
    totals, (out_prefix, out_actions, grad_prefix, grad_actions) = lax.scan(one_item, zero_grads, (prefix_tokens, actions, robot_state, text_len, flow_index, grad_pre, grad_act))
    return (out_prefix, out_actions, grad_prefix, grad_actions, totals[0], totals[1], totals[2], totals[3], totals[4], totals[5], totals[6], totals[7], totals[8], totals[9], totals[10], totals[11], totals[12], totals[13], totals[14], totals[15], totals[16], totals[17], totals[18], totals[19], totals[20], totals[21])
```

```python
import math

import jax
import jax.numpy as jnp
from jax import lax
from jax.sharding import PartitionSpec as P

DS = 1024
HEADS = 8
HD = 256
CAMS = 3
PATCH = 192
NTIME = 1000
AXES = ("dp", "ctx")

masked_score = -1e30
F32 = jnp.float32
BF16 = jnp.bfloat16


def rms_norm(values, norm_gain):
    return values * lax.rsqrt(jnp.mean(values * values, axis=-1, keepdims=True) + 1e-06) * norm_gain


def norm_back(values, norm_gain, cotangent):
    _, pullback = jax.vjp(rms_norm, values, norm_gain)
    return pullback(cotangent)


def time_embed(sample_index):
    flow_time = (sample_index.astype(F32) + 0.5) / NTIME
    halves = DS // 2
    fraction = jnp.arange(halves, dtype=F32) / (halves - 1)
    period = 0.004 * jnp.power(1000.0, fraction)
    angles = 2.0 * math.pi * flow_time[..., None] / period
    return jnp.concatenate([jnp.sin(angles), jnp.cos(angles)], axis=-1)


def mm(left, right):
    return jnp.dot(left, right, preferred_element_type=F32)


def mm_tr(left, right):
    return lax.dot_general(left, right, (((1,), (1,)), ((), ())), preferred_element_type=F32)


def outer_sum(left, right):
    return lax.dot_general(left, right, (((0,), (0,)), ((), ())), preferred_element_type=F32)


def ein(spec, left, right):
    return jnp.einsum(spec, left, right, preferred_element_type=F32)


def add_low(left, right):
    return (left.astype(F32) + right.astype(F32)).astype(BF16)


def gate(array, *after):
    return lax.optimization_barrier((array,) + after)[0]


def pad_rows(array, rows):
    return jnp.pad(array, ((0, rows - array.shape[0]), (0, 0)))


def gated_unit(gate_value, up_value):
    return jax.nn.gelu(gate_value, approximate=True) * up_value


def make_body(n, q):
    m = 4 if n >= 8 else n // 2
    high = n // (2 * m)

    def flat(dp, ctx):
        return dp * q + ctx

    def xor_pairs(dp_mask, ctx_mask):
        return [(flat(d, c), flat(d ^ dp_mask, c ^ ctx_mask)) for d in range(n) for c in range(q)]

    swap_c = xor_pairs(0, 1)
    swap_y = xor_pairs(0, 2)
    swap_x = xor_pairs(1, 0)
    swap_high = [xor_pairs(2 * m * 2**i, 0) for i in range(high.bit_length() - 1)]

    def z_step(step, low, end):
        return [
            (flat((h * m + z) * 2 + x, c), flat((h * m + z + step) * 2 + x, c))
            for h in range(high)
            for z in range(low, end)
            for x in range(2)
            for c in range(q)
        ]

    def send(array, pairs):
        return lax.ppermute(array, AXES, pairs)

    def z_xor(array, k):
        return send(array, xor_pairs(2 * k, 0))

    def pick(pieces, index):
        out = pieces[-1]
        for k in range(len(pieces) - 2, -1, -1):
            out = jnp.where(index == k, pieces[k], out)
        return out

    def in_order(bit, mine, other, axis):
        return jnp.where(bit == 0, jnp.stack([mine, other], axis), jnp.stack([other, mine], axis))

    def gather_rows(own, z):
        ups, downs = [], []
        up = down = own
        for s in range(1, m):
            up = send(up, z_step(1, s - 1, m - 1))
            down = send(down, z_step(-1, 1, m - s + 1))
            ups.append(up)
            downs.append(down)
        slots = [own]
        for s in range(1, m):
            slots.append(jnp.where(z + s < m, downs[s - 1], ups[m - s - 1]))
        out = []
        for pair in ((0, 2), (1, 3)):
            near = jnp.concatenate([slots[s] for s in pair])
            near = jnp.concatenate([near, send(near, swap_y)])
            out.append((near, send(near, swap_c)))
        return out

    def scatter_rows(even, odd, rows):
        mine = {}
        for pair, (near, far) in (((1, 3), odd), ((0, 2), even)):
            near = add_low(near, send(far, swap_c))
            near = add_low(near[: 2 * rows], send(near[2 * rows :], swap_y))
            mine[pair[0]], mine[pair[1]] = near[:rows], near[rows:]
        up = down = None
        for s in range(m - 1, 0, -1):
            above = mine[s] if up is None else add_low(mine[s], up)
            up = send(above, z_step(1, 0, m - s))
            below = mine[m - s] if down is None else add_low(mine[m - s], down)
            down = send(below, z_step(-1, s, m))
        return mine[0].astype(F32) + up.astype(F32) + down.astype(F32), up

    def gather_ctx(own):
        pair = jnp.stack([own, send(own, swap_y)])
        return jnp.concatenate([pair, send(pair, swap_c)])

    def scatter_ctx(parts):
        pair = add_low(parts[:2], send(parts[2:], swap_c))
        return pair[0].astype(F32) + send(pair[1], swap_y).astype(F32)

    def gather_light(own, parts, place, after):
        z, x, y, c, highs = place
        pieces = [own] + [z_xor(own, k) for k in range(1, m)]
        lines = jnp.stack([pick(pieces, z ^ t) for t in range(m)])
        for bit, pairs in zip(highs, swap_high, strict=True):
            lines = in_order(bit, lines, send(lines, pairs), 0)
        lines = lines.reshape((high * m,) + own.shape)
        if after:
            lines = gate(lines, *after)
        out, last = [], []
        start = 0
        for at, size in enumerate(parts):
            cut = lines[:, :, start : start + size]
            start += size
            if at % 2 == 0:
                cut = in_order(y, cut, send(cut, swap_y), 1)
                got = send(cut, swap_x)
                cut = in_order(x, cut, got, 1)
            else:
                cut = in_order(x, cut, send(cut, swap_x), 1)
                got = send(cut, swap_y)
                cut = in_order(y, cut, got, 2)
            last.append(got)
            cut = in_order(c, cut, send(cut, swap_c), 3)
            out.append(cut.reshape(n * q * own.shape[0], size))
        return out, pieces[1:], last

    def scatter_light(parts, place):
        z, x, y, c, highs = place

        out = []
        for at, part in enumerate(parts):
            rows = part.shape[0] // (n * q)
            part = fold(part.reshape(high * m, 2, 2, 2, rows, part.shape[1]), c, swap_c, 3)
            if at % 2 == 0:
                part = fold(fold(part, x, swap_x, 1), y, swap_y, 1)
            else:
                part = fold(fold(part, y, swap_y, 2), x, swap_x, 1)
            for bit, pairs in zip(reversed(highs), reversed(swap_high), strict=True):
                part = fold(part.reshape((2, -1) + part.shape[1:]), bit, pairs, 0)
            total = lax.dynamic_index_in_dim(part, z, 0, keepdims=False).astype(F32)
            for k in range(1, m):
                piece = lax.dynamic_index_in_dim(part, z ^ k, 0, keepdims=False)
                total = total + z_xor(piece, k).astype(F32)
            out.append(total)
        return out

    def narrowed(array):
        size = array.shape[-1] // high
        return jnp.concatenate([array[..., i * size : (i + 1) * size] for i in range(high)], axis=-2)

    def widened(array):
        size = array.shape[-2] // high
        return jnp.concatenate([array[..., i * size : (i + 1) * size, :] for i in range(high)], axis=-1)

    def cut(array, index, size, axis):
        return lax.dynamic_slice_in_dim(array, index * size, size, axis)

    def gather_ffn(gate_pre, up_pre, down_pre, gate_act, up_act, down_act, place, after_z, after_x):
        z, x, _, _, highs = place
        w = gate_pre.shape[0]
        cols = gate_pre.shape[1] // m
        w_act = gate_act.shape[0]
        cols_act = gate_act.shape[1] // m
        flat_act = high * w_act

        def exchange(piece_of, after):
            pieces = [piece_of(z)]
            for k in range(1, m):
                pieces.append(z_xor(gate(piece_of(z ^ k), *after), k))
            return pieces

        def down_piece(t):
            last = cut(down_act, t, cols_act, 0)
            return jnp.concatenate(
                [
                    cut(down_pre, t, cols, 0),
                    narrowed(cut(gate_act, t, cols_act, 1)),
                    narrowed(cut(up_act, t, cols_act, 1)),
                    jnp.concatenate([last[: cols_act // 2], last[cols_act // 2 :]], axis=1),
                ],
                axis=0,
            )

        downs = exchange(down_piece, after_z)
        gates = exchange(lambda t: cut(gate_pre, t, cols, 1), downs[1:])
        ups = exchange(lambda t: cut(up_pre, t, cols, 1), gates[1:])

        near = jnp.concatenate([pick(downs, z ^ t) for t in range(m)], axis=1)
        far = send(gate(near, *after_x), swap_x)
        blocks = []
        for t in range(m):
            a, b = near[:, t * w : (t + 1) * w], far[:, t * w : (t + 1) * w]
            blocks += [jnp.where(x == 0, a, b), jnp.where(x == 0, b, a)]
        down_full = jnp.concatenate(blocks, axis=1)
        for bit, pairs in zip(highs, swap_high, strict=True):
            other = send(down_full, pairs)
            down_full = jnp.concatenate(
                [jnp.where(bit == 0, down_full, other), jnp.where(bit == 0, other, down_full)], axis=1
            )

        def rows_of(pieces, after):
            lines = jnp.stack([pick(pieces, z ^ t) for t in range(m)])
            got = send(gate(lines, *after), swap_x)
            full = in_order(x, lines, got, 1).reshape(1, 2 * m * w, cols)
            for bit, pairs in zip(highs, swap_high, strict=True):
                full = in_order(bit, full, send(full, pairs), 0).reshape(1, -1, cols)
            return full.reshape(n * w, cols), got

        gate_full, got = rows_of(gates, (far,))
        up_full, _ = rows_of(ups, (got,))
        narrow = down_full[:cols]

        def rows_act(start):
            part = down_full[start : start + flat_act]
            return jnp.concatenate([widened(part[:, d * w : (d + 1) * w]) for d in range(n)])

        wide_act = (rows_act(cols), rows_act(cols + flat_act))
        last = down_full[cols + 2 * flat_act :]
        narrow_act = jnp.concatenate(
            [
                jnp.concatenate([last[:, d * w : d * w + w_act], last[:, d * w + w_act : (d + 1) * w]])
                for d in range(n)
            ],
            axis=1,
        )
        return (gate_full, up_full), narrow, wide_act, narrow_act, ups[1:]

    def fold(array, bit, pairs, axis):
        theirs = lax.dynamic_index_in_dim(array, 1 - bit, axis, keepdims=False)
        mine = lax.dynamic_index_in_dim(array, bit, axis, keepdims=False)
        return add_low(mine, send(theirs, pairs))

    def scatter_ffn_rows(total, place, after):
        z, x, _, _, highs = place
        part = fold(total.reshape(n // 2, 2, total.shape[0] // n, total.shape[1]), x, swap_x, 1)
        for bit, pairs in zip(reversed(highs), reversed(swap_high), strict=True):
            part = fold(part.reshape((2, -1) + part.shape[1:]), bit, pairs, 0)
        part = gate(part, *after)
        pieces = []
        for k in range(m):
            piece = lax.dynamic_index_in_dim(part, z ^ k, 0, keepdims=False)
            pieces.append(piece if k == 0 else z_xor(piece, k))
        return [pick(pieces, z ^ t) for t in range(m)], pieces[1:]

    def scatter_ffn_columns(total, place, after):
        z, x, _, _, highs = place
        w = total.shape[1] // n
        for bit, pairs in zip(reversed(highs), reversed(swap_high), strict=True):
            half = total.shape[1] // 2
            theirs = jnp.where(bit == 0, total[:, half:], total[:, :half])
            mine = jnp.where(bit == 0, total[:, :half], total[:, half:])
            total = add_low(mine, send(theirs, pairs))
        blocks = [total[:, d * w : (d + 1) * w] for d in range(2 * m)]
        theirs = [jnp.where(x == 0, blocks[2 * t + 1], blocks[2 * t]) for t in range(m)]
        mine = [jnp.where(x == 0, blocks[2 * t], blocks[2 * t + 1]) for t in range(m)]
        got = send(jnp.concatenate(theirs, axis=1), swap_x)
        mine = [add_low(mine[t], got[:, t * w : (t + 1) * w]) for t in range(m)]
        mine[0] = gate(mine[0], *after)
        pieces = []
        for k in range(m):
            piece = pick(mine, z ^ k)
            pieces.append(piece if k == 0 else z_xor(piece, k))
        return [pick(pieces, z ^ t) for t in range(m)], pieces[1:]

    def ffn_unit(rows, wide, narrow):
        gate_value, up_value = mm(rows, wide[0]), mm(rows, wide[1])
        hidden = gated_unit(gate_value, up_value).astype(BF16)
        return gate_value, up_value, hidden, mm(hidden, narrow).astype(BF16)

    def ffn_back(d_hidden, gate_value, up_value, wide):
        _, pullback = jax.vjp(gated_unit, gate_value, up_value)
        d_gate, d_up = pullback(d_hidden)
        d_gate, d_up = d_gate.astype(BF16), d_up.astype(BF16)
        d_rows = (mm_tr(d_gate, wide[0]) + mm_tr(d_up, wide[1])).astype(BF16)
        return d_rows, d_gate, d_up

    def per_device(
        prefix_tokens,
        actions,
        robot_state,
        text_len,
        flow_index,
        query_pre,
        key_pre,
        value_pre,
        out_pre,
        gain_attn_pre,
        gain_ffn_pre,
        query_act,
        key_act,
        value_act,
        out_act,
        gain_attn_act,
        gain_ffn_act,
        action_in,
        mix_first,
        mix_second,
        state_in,
        gate_pre,
        up_pre,
        down_pre,
        gate_act,
        up_act,
        down_act,
        grad_pre,
        grad_act,
    ):
        dp = lax.axis_index("dp")
        ctx = lax.axis_index("ctx")
        z, x = (dp // 2) % m, dp % 2
        y, c = ctx // 2, ctx % 2
        highs = [(dp // (2 * m * 2**i)) % 2 for i in range(len(swap_high))]
        place = (z, x, y, c, highs)
        width = prefix_tokens.shape[2]
        tokens = prefix_tokens.shape[1]
        rows_pre = -(-tokens // 32) * 32
        suffix = grad_act.shape[2]
        rows_act = -(-suffix // 32) * 32
        acts = actions.shape[2]
        devices = n * q
        r64, r32 = query_pre.shape[0], query_act.shape[0]

        pad = jnp.zeros((r64 - r32,), BF16)
        gains = jnp.stack(
            [
                gain_attn_pre,
                gain_ffn_pre,
                jnp.concatenate([gain_attn_act, pad]),
                jnp.concatenate([gain_ffn_act, pad]),
            ],
            axis=1,
        )
        gains = jnp.pad(gains, ((0, 0), (0, 124)))
        first = jnp.concatenate([query_pre, key_pre, value_pre, gains], axis=1)
        small = jnp.pad(jnp.concatenate([action_in, state_in], axis=1), ((0, 0), (0, 64)))
        third = jnp.concatenate(
            [query_act, key_act, value_act, mix_second, mix_first[:r32], mix_first[r32:], small], axis=1
        )
        second = jnp.concatenate([out_pre, out_act], axis=1)
        third = lax.all_gather(third, AXES, axis=0, tiled=True)
        half = width // 2 + HD
        (first_a, first_b), first_z, first_x = gather_light(first, (half, half + 128), place, ())
        (out_a, out_b), out_z, out_x = gather_light(
            gate(second, *first_z), (width, out_act.shape[1]), place, tuple(first_x)
        )
        qkv_w = jnp.concatenate([first_a, first_b[:, :half]], axis=1)
        gain_rows = first_b[:, half:].astype(F32)
        norm_attn, norm_ffn = gain_rows[:, 0], gain_rows[:, 1]
        gain_small = gain_rows[:, 2:4].reshape(devices, r64, 2)[:, :r32].reshape(devices * r32, 2)
        norm_attn_act, norm_ffn_act = gain_small[:, 0], gain_small[:, 1]
        qkv_act_w = third[:, : width + 2 * HD]
        at = width + 2 * HD
        mixer_second = third[:, at : at + DS]
        mixer_first = (
            third[:, at + DS : at + 3 * DS]
            .reshape(devices, r32, 2, DS)
            .transpose(0, 2, 1, 3)
            .reshape(2 * DS, DS)
        )
        action_full = third[:, at + 3 * DS : at + 3 * DS + 32]
        state_full = third[:, at + 3 * DS + 32 : at + 3 * DS + 64]
        out_w, out_act_w = out_a, out_b

        wide, narrow, wide_act, narrow_act, ffn_z = gather_ffn(
            gate_pre, up_pre, down_pre, gate_act, up_act, down_act, place, tuple(out_z), tuple(out_x)
        )
        sharing = [
            [flat((h * m + a) * 2 + b, d) for a in range(m) for d in range(q)]
            for h in range(high)
            for b in range(2)
        ]

        def gather_act(block):
            return lax.all_gather(block, AXES, axis=0, tiled=True, axis_index_groups=sharing)

        def scatter_act(block):
            return lax.psum_scatter(
                block, AXES, scatter_dimension=0, tiled=True, axis_index_groups=sharing
            ).astype(F32)

        (cot_e0, cot_e1), (cot_o0, cot_o1) = gather_rows(
            gate(pad_rows(grad_pre[0], rows_pre), *ffn_z), z
        )
        cot_all_act = gather_act(pad_rows(grad_act[0, 0], rows_act))

        time_rows = time_embed(flow_index[0, 0])
        action_emb = mm_tr(actions[0, 0], action_full)
        mix_input = jnp.concatenate(
            [action_emb, jnp.broadcast_to(time_rows[None, :], action_emb.shape)], axis=-1
        ).astype(BF16)
        pre_mix = mm(mix_input, mixer_first)
        mixed_act = jax.nn.silu(pre_mix).astype(BF16)
        action_rows = mm(mixed_act, mixer_second)
        state_row = mm_tr(robot_state, state_full)
        side_input = pad_rows(jnp.concatenate([state_row, action_rows], axis=0), rows_act)

        prefix_in = pad_rows(prefix_tokens[0], rows_pre).astype(F32)
        normed_pre = rms_norm(prefix_in, norm_attn).astype(BF16)
        normed_act = rms_norm(side_input, norm_attn_act).astype(BF16)
        qkv_pre = mm(normed_pre, qkv_w).astype(BF16)
        qkv_act = mm(normed_act, qkv_act_w).astype(BF16)
        queries_pre = qkv_pre[:, :width].reshape(rows_pre, HEADS, HD)
        queries_act = qkv_act[:, :width].reshape(rows_act, HEADS, HD)
        keys_act = qkv_act[:, width : width + HD]
        values_act = qkv_act[:, width + HD :]
        both_kv = gather_ctx(qkv_pre[:, width:]).reshape(q * rows_pre, 2 * HD)
        keys, values = both_kv[:, :HD], both_kv[:, HD:]
        key_count = q * rows_pre

        order = jnp.array([0, 2, 1, 3])
        spot = jnp.arange(rows_pre)
        positions = (ctx ^ order)[:, None] * tokens + spot[None, :]
        camera_rows = CAMS * PATCH
        key_valid = (positions < camera_rows) | (positions - camera_rows < text_len[0])
        key_valid = (key_valid & (spot < tokens)[None, :]).reshape(-1)
        scale = HD ** (-0.5)

        def prefix_scores():
            scores = ein("qhd,kd->hqk", queries_pre, keys) * scale
            return jnp.where(key_valid[None, None, :], scores, masked_score)

        groups = jnp.arange(rows_act) > 0
        own_block = (groups[None, :] <= groups[:, None]) & (jnp.arange(rows_act) < suffix)[None, :]

        def side_scores():
            far = ein("qhd,kd->hqk", queries_act, keys) * scale
            far = jnp.where(key_valid[None, None, :], far, masked_score)
            near = ein("qhd,kd->hqk", queries_act, keys_act) * scale
            near = jnp.where(own_block[None], near, masked_score)
            return jnp.concatenate([far, near], axis=-1)

        def soft_rows(scores):
            highest = jnp.max(scores, axis=-1, keepdims=True)
            totals = jnp.sum(jnp.exp(scores - highest), axis=-1, keepdims=True)
            log_total = highest + jnp.log(totals)
            return jnp.exp(scores - log_total), log_total

        probs_pre, total_pre = soft_rows(prefix_scores())
        attn_pre = ein("hqk,kd->qhd", probs_pre.astype(BF16), values)
        attn_pre = attn_pre.reshape(rows_pre, width).astype(BF16)
        probs_act, total_act = soft_rows(side_scores())
        probs_act_low = probs_act.astype(BF16)
        attn_act = ein("hqk,kd->qhd", probs_act_low[..., :key_count], values) + ein(
            "hqk,kd->qhd", probs_act_low[..., key_count:], values_act
        )
        attn_act = attn_act.reshape(rows_act, width).astype(BF16)
        mid_pre = prefix_in + mm(attn_pre, out_w)
        mid_act = side_input + mm(attn_act, out_act_w)
        normed_two_pre = rms_norm(mid_pre, norm_ffn).astype(BF16)
        normed_two_act = rms_norm(mid_act, norm_ffn_act).astype(BF16)

        (row_e0, row_e1), (row_o0, row_o1) = gather_rows(normed_two_pre, z)
        rows = (row_o1, row_o0, row_e1, row_e0)
        cots = (cot_o1, cot_o0, cot_e1, cot_e0)
        rows_all_act = gather_act(normed_two_act)
        units = [ffn_unit(r, wide, narrow) for r in rows]
        gate_act_value, up_act_value, hidden_act, part_act = ffn_unit(rows_all_act, wide_act, narrow_act)
        parts = [unit[3] for unit in units]
        branch, branch_last = scatter_rows((parts[3], parts[2]), (parts[1], parts[0]), rows_pre)
        out_prefix = (mid_pre + branch)[:tokens]
        out_actions = (mid_act + scatter_act(part_act))[:suffix]

        backs = [
            ffn_back(mm_tr(cot, narrow), unit[0], unit[1], wide)
            for cot, unit in zip(cots, units, strict=True)
        ]
        d_branch, d_last = scatter_rows((backs[3][0], backs[2][0]), (backs[1][0], backs[0][0]), rows_pre)
        d_rows_act, d_gate_act, d_up_act = ffn_back(
            mm_tr(cot_all_act, narrow_act), gate_act_value, up_act_value, wide_act
        )
        d_branch_act = scatter_act(d_rows_act)

        cols_act = gate_act.shape[1] // m
        w_act = gate_act.shape[0]
        w = gate_pre.shape[0]
        cols = gate_pre.shape[1] // m
        flat_act = high * w_act
        rows_join = jnp.concatenate(rows)
        grad_down_act = outer_sum(hidden_act, cot_all_act).astype(BF16)
        half_act = cols_act // 2

        def blocks_act(total):
            return jnp.concatenate(
                [narrowed(total[d * w_act : (d + 1) * w_act]) for d in range(n)], axis=1
            )

        narrow_parts = jnp.concatenate(
            [
                outer_sum(jnp.concatenate([unit[2] for unit in units]), jnp.concatenate(cots)).astype(BF16),
                blocks_act(outer_sum(rows_all_act, d_gate_act).astype(BF16)),
                blocks_act(outer_sum(rows_all_act, d_up_act).astype(BF16)),
                jnp.concatenate(
                    [
                        grad_down_act[at : at + half_act, d * w_act : (d + 1) * w_act]
                        for d in range(n)
                        for at in (0, half_act)
                    ],
                    axis=1,
                ),
            ],
            axis=0,
        )
        grad_gate = outer_sum(rows_join, jnp.concatenate([back[1] for back in backs])).astype(BF16)
        grad_up = outer_sum(rows_join, jnp.concatenate([back[2] for back in backs])).astype(BF16)
        down_got, down_z = scatter_ffn_columns(narrow_parts, place, (d_last,))
        gate_got, gate_z = scatter_ffn_rows(grad_gate, place, tuple(down_z))
        up_got, _ = scatter_ffn_rows(grad_up, place, tuple(gate_z))

        def beside(pieces):
            return jnp.concatenate(pieces, axis=1).astype(F32)

        grad_gate_pre = beside(gate_got)
        grad_up_pre = beside(up_got)
        grad_down_pre = jnp.concatenate([g[:cols] for g in down_got]).astype(F32)
        grad_gate_act = beside([widened(g[cols : cols + flat_act]) for g in down_got])
        grad_up_act = beside([widened(g[cols + flat_act : cols + 2 * flat_act]) for g in down_got])
        last = [g[cols + 2 * flat_act :] for g in down_got]
        grad_down_act = jnp.concatenate([g[:, at : at + w_act] for g in last for at in (0, w_act)])
        grad_down_act = grad_down_act.astype(F32)

        d_mid_pre, grad_norm_ffn = norm_back(mid_pre, norm_ffn, d_branch)
        d_mid_pre = d_mid_pre + pad_rows(grad_pre[0], rows_pre).astype(F32)
        d_mid_act, grad_norm_ffn_act = norm_back(mid_act, norm_ffn_act, d_branch_act)
        d_mid_act = d_mid_act + pad_rows(grad_act[0, 0], rows_act).astype(F32)
        d_mid_low = d_mid_pre.astype(BF16)
        d_mid_act_low = d_mid_act.astype(BF16)
        grad_out_pre = outer_sum(attn_pre, d_mid_low).astype(BF16)
        grad_out_act = outer_sum(attn_act, d_mid_act_low).astype(BF16)
        got_second = lax.psum_scatter(
            jnp.concatenate([grad_out_pre, grad_out_act], axis=1), AXES, scatter_dimension=0, tiled=True
        ).astype(F32)

        d_attn_pre = mm_tr(d_mid_low, out_w).astype(BF16).reshape(rows_pre, HEADS, HD)
        d_attn_act = mm_tr(d_mid_act_low, out_act_w).astype(BF16).reshape(rows_act, HEADS, HD)
        probs_pre = jnp.exp(prefix_scores() - total_pre)
        d_probs = ein("qhd,kd->hqk", d_attn_pre, values)
        d_scores = probs_pre * (d_probs - jnp.sum(probs_pre * d_probs, axis=-1, keepdims=True))
        d_scores = d_scores.astype(BF16)
        d_query_pre = (ein("hqk,kd->qhd", d_scores, keys) * scale).reshape(rows_pre, width).astype(BF16)
        key_terms = ein("hqk,qhd->kd", d_scores, queries_pre)
        value_terms = ein("hqk,qhd->kd", probs_pre.astype(BF16), d_attn_pre)

        probs_act = jnp.exp(side_scores() - total_act)
        probs_act_low = probs_act.astype(BF16)
        d_probs_act = jnp.concatenate(
            [ein("qhd,kd->hqk", d_attn_act, values), ein("qhd,kd->hqk", d_attn_act, values_act)], axis=-1
        )
        d_scores_act = probs_act * (
            d_probs_act - jnp.sum(probs_act * d_probs_act, axis=-1, keepdims=True)
        )
        d_scores_act = d_scores_act.astype(BF16)
        far, near = d_scores_act[..., :key_count], d_scores_act[..., key_count:]
        d_query_act = ein("hqk,kd->qhd", far, keys) + ein("hqk,kd->qhd", near, keys_act)
        d_query_act = (d_query_act * scale).reshape(rows_act, width).astype(BF16)
        key_terms = (key_terms + ein("hqk,qhd->kd", far, queries_act)) * scale
        value_terms = value_terms + ein("hqk,qhd->kd", probs_act_low[..., :key_count], d_attn_act)
        d_keys_act = (ein("hqk,qhd->kd", near, queries_act) * scale).astype(BF16)
        d_values_act = ein("hqk,qhd->kd", probs_act_low[..., key_count:], d_attn_act).astype(BF16)
        kv_terms = jnp.concatenate([key_terms, value_terms], axis=1).astype(BF16)
        d_kv = scatter_ctx(kv_terms.reshape(q, rows_pre, 2 * HD)).astype(BF16)

        d_qkv_pre = jnp.concatenate([d_query_pre, d_kv], axis=1)
        d_qkv_act = jnp.concatenate([d_query_act, d_keys_act, d_values_act], axis=1)
        d_normed_pre = mm_tr(d_qkv_pre, qkv_w)
        d_normed_act = mm_tr(d_qkv_act, qkv_act_w)
        grad_qkv_pre = outer_sum(normed_pre, d_qkv_pre).astype(BF16)
        grad_qkv_act = outer_sum(normed_act, d_qkv_act).astype(BF16)
        grad_prefix, grad_norm_attn = norm_back(prefix_in, norm_attn, d_normed_pre)
        grad_prefix = (grad_prefix + d_mid_pre)[:tokens]
        d_side, grad_norm_attn_act = norm_back(side_input, norm_attn_act, d_normed_act)
        d_side = d_side + d_mid_act
        grad_state_in = outer_sum(d_side[:1].astype(BF16), robot_state)
        d_action_rows = d_side[1 : 1 + acts].astype(BF16)
        grad_mix_second = outer_sum(mixed_act, d_action_rows).astype(BF16)
        d_mixed = mm_tr(d_action_rows, mixer_second)
        _, silu_back = jax.vjp(jax.nn.silu, pre_mix)
        d_pre_mix = silu_back(d_mixed)[0].astype(BF16)
        grad_mix_first = outer_sum(mix_input, d_pre_mix).astype(BF16)
        d_action_emb = mm_tr(d_pre_mix, mixer_first[:DS]).astype(BF16)
        grad_action_in = outer_sum(d_action_emb, actions[0, 0])
        grad_actions = mm(d_action_emb, action_full)

        act_gains = jnp.stack([grad_norm_attn_act, grad_norm_ffn_act], axis=1).reshape(devices, r32, 2)
        act_gains = jnp.pad(act_gains, ((0, 0), (0, r64 - r32), (0, 0))).reshape(devices * r64, 2)
        gain_grads = jnp.concatenate(
            [jnp.stack([grad_norm_attn, grad_norm_ffn], axis=1), act_gains], axis=1
        ).astype(BF16)
        gain_grads = jnp.pad(gain_grads, ((0, 0), (0, 124)))
        got_first = scatter_light(
            [grad_qkv_pre[:, :half], jnp.concatenate([grad_qkv_pre[:, half:], gain_grads], axis=1)], place
        )
        got_first = jnp.concatenate(got_first, axis=1)
        small_grads = jnp.pad(
            jnp.concatenate([grad_action_in, grad_state_in], axis=1).astype(BF16), ((0, 0), (0, 64))
        )
        mix_first_rows = (
            grad_mix_first.reshape(devices, 2, r32, DS).transpose(0, 2, 1, 3).reshape(devices * r32, 2 * DS)
        )
        mixes = jnp.concatenate([grad_mix_second, mix_first_rows, small_grads], axis=1)
        got_third = jnp.concatenate(scatter_light([grad_qkv_act, mixes], place), axis=1)

        wide_end = width + 2 * HD
        tail = got_third[:, at + 3 * DS :]
        return (
            out_prefix[None],
            out_actions[None, None],
            grad_prefix[None],
            grad_actions[None, None],
            got_first[:, :width],
            got_first[:, width : width + HD],
            got_first[:, width + HD : wide_end],
            got_second[:, :width],
            got_first[:, wide_end],
            got_first[:, wide_end + 1],
            got_third[:, :width],
            got_third[:, width : width + HD],
            got_third[:, width + HD : wide_end],
            got_second[:, width:],
            got_first[:r32, wide_end + 2],
            got_first[:r32, wide_end + 3],
            tail[:, :32],
            jnp.concatenate([got_third[:, at + DS : at + 2 * DS], got_third[:, at + 2 * DS : at + 3 * DS]]),
            got_third[:, at : at + DS],
            tail[:, 32:64],
            grad_gate_pre,
            grad_up_pre,
            grad_down_pre,
            grad_gate_act,
            grad_up_act,
            grad_down_act,
        )

    return per_device


def solution(mesh):
    rows = P(("dp", "ctx"), None)
    line = P(("dp", "ctx"))
    return jax.shard_map(
        make_body(mesh.shape["dp"], mesh.shape["ctx"]),
        mesh=mesh,
        in_specs=(
            P("dp", "ctx", None),
            P("dp", "ctx", None, None),
            P("dp", None),
            P("dp"),
            P("dp", "ctx"),
            rows,
            rows,
            rows,
            rows,
            line,
            line,
            rows,
            rows,
            rows,
            rows,
            line,
            line,
            rows,
            rows,
            rows,
            rows,
            P("dp", "ctx"),
            P("dp", "ctx"),
            P("ctx", "dp"),
            P("dp", "ctx"),
            P("dp", "ctx"),
            P("ctx", "dp"),
            P("dp", "ctx", None),
            P("dp", "ctx", None, None),
        ),
        out_specs=(
            P("dp", "ctx", None),
            P("dp", "ctx", None, None),
            P("dp", "ctx", None),
            P("dp", "ctx", None, None),
            rows,
            rows,
            rows,
            rows,
            line,
            line,
            rows,
            rows,
            rows,
            rows,
            line,
            line,
            rows,
            rows,
            rows,
            rows,
            P("dp", "ctx"),
            P("dp", "ctx"),
            P("ctx", "dp"),
            P("dp", "ctx"),
            P("dp", "ctx"),
            P("ctx", "dp"),
        ),
        check_vma=False,
    )
```

```python
import math

import jax
import jax.numpy as jnp
from jax import lax
from jax.experimental import pallas as pl
from jax.experimental.pallas import tpu as pltpu
from jax.sharding import PartitionSpec as P

DS = 1024
HEADS = 8
HD = 256
CAMS = 3
PATCH = 192
NTIME = 1000
AXES = ("dp", "ctx")

masked_score = -1e30
F32 = jnp.float32
BF16 = jnp.bfloat16


def rms_norm(values, norm_gain):
    return values * lax.rsqrt(jnp.mean(values * values, axis=-1, keepdims=True) + 1e-06) * norm_gain


def norm_back(values, norm_gain, cotangent):
    _, pullback = jax.vjp(rms_norm, values, norm_gain)
    return pullback(cotangent)


def time_embed(sample_index):
    flow_time = (sample_index.astype(F32) + 0.5) / NTIME
    halves = DS // 2
    fraction = jnp.arange(halves, dtype=F32) / (halves - 1)
    period = 0.004 * jnp.power(1000.0, fraction)
    angles = 2.0 * math.pi * flow_time[..., None] / period
    return jnp.concatenate([jnp.sin(angles), jnp.cos(angles)], axis=-1)


def mm(left, right):
    return jnp.dot(left, right, preferred_element_type=F32)


def mm_tr(left, right):
    return lax.dot_general(left, right, (((1,), (1,)), ((), ())), preferred_element_type=F32)


def outer_sum(left, right):
    return lax.dot_general(left, right, (((0,), (0,)), ((), ())), preferred_element_type=F32)


def ein(spec, left, right):
    return jnp.einsum(spec, left, right, preferred_element_type=F32)


def add_low(left, right):
    return (left.astype(F32) + right.astype(F32)).astype(BF16)


def sync(*arrays):
    return lax.optimization_barrier(arrays)


def together(groups):
    flat = sync(*[array for group in groups for array in group])
    out, at = [], 0
    for group in groups:
        out.append(list(flat[at : at + len(group)]))
        at += len(group)
    return out


def pad_rows(array, rows):
    return jnp.pad(array, ((0, rows - array.shape[0]), (0, 0)))


def gated_unit(gate_value, up_value):
    return jax.nn.gelu(gate_value, approximate=True) * up_value


VMEM_BYTES = 40 * 2**20


def outer_kernel(count, *refs):
    left, right, out_ref = refs[:count], refs[count : 2 * count], refs[2 * count]
    total = None
    for one, other in zip(left, right, strict=True):
        part = lax.dot_general(one[...], other[...], (((0,), (0,)), ((), ())), preferred_element_type=F32)
        total = part if total is None else total + part
    out_ref[...] = total.astype(BF16)


def outer_sums(lefts, rights, tile=256):
    count, rows = len(lefts), lefts[0].shape[0]
    height, width = lefts[0].shape[1], rights[0].shape[1]
    return pl.pallas_call(
        lambda *refs: outer_kernel(count, *refs),
        grid=(height // tile,),
        in_specs=[pl.BlockSpec((rows, tile), lambda i: (0, i))] * count
        + [pl.BlockSpec((rows, width), lambda i: (0, 0))] * count,
        out_specs=pl.BlockSpec((tile, width), lambda i: (i, 0)),
        out_shape=jax.ShapeDtypeStruct((height, width), BF16),
        compiler_params=pltpu.CompilerParams(vmem_limit_bytes=VMEM_BYTES),
        cost_estimate=pl.CostEstimate(
            flops=2 * count * rows * height * width,
            bytes_accessed=2 * count * rows * (height + width) + 2 * height * width,
            transcendentals=0,
        ),
    )(*lefts, *rights)


def make_body(n, q):
    m = 4 if n >= 8 else n // 2
    high = n // (2 * m)

    def flat(dp, ctx):
        return dp * q + ctx

    def xor_pairs(dp_mask, ctx_mask):
        return [(flat(d, c), flat(d ^ dp_mask, c ^ ctx_mask)) for d in range(n) for c in range(q)]

    swap_c = xor_pairs(0, 1)
    swap_y = xor_pairs(0, 2)
    swap_x = xor_pairs(1, 0)
    swap_high = [xor_pairs(2 * m * 2**i, 0) for i in range(high.bit_length() - 1)]

    lines_z = [
        [flat((h * m + z) * 2 + x, c) for z in range(m)] for h in range(high) for x in range(2) for c in range(q)
    ]

    def send(array, pairs):
        return lax.ppermute(array, AXES, pairs)

    def z_swap(parts):
        return lax.all_to_all(parts, AXES, 0, 0, axis_index_groups=lines_z)

    def z_gather(own):
        return z_swap(jnp.broadcast_to(own[None], (m,) + own.shape))

    def in_order(bit, mine, other, axis):
        return jnp.where(bit == 0, jnp.stack([mine, other], axis), jnp.stack([other, mine], axis))

    def with_highs(lines, place):
        lines = lines[None]
        for bit, pairs in zip(place[4], swap_high, strict=True):
            lines = in_order(bit, lines, send(lines, pairs), 0)
            lines = lines.reshape((-1,) + lines.shape[2:])
        return lines.reshape((-1,) + lines.shape[2:])

    def down_piece(down_pre, gate_act, up_act, down_act):
        cols = down_pre.shape[0] // m
        cols_act = gate_act.shape[1] // m

        def piece_of(t):
            last = cut(down_act, t, cols_act, 0)
            return jnp.concatenate(
                [
                    cut(down_pre, t, cols, 0),
                    narrowed(cut(gate_act, t, cols_act, 1)),
                    narrowed(cut(up_act, t, cols_act, 1)),
                    jnp.concatenate([last[: cols_act // 2], last[cols_act // 2 :]], axis=1),
                ],
                axis=0,
            )

        return piece_of

    def columns_full(near, far, place):
        x, highs = place[1], place[4]
        blocks = []
        for t in range(m):
            blocks += [jnp.where(x == 0, near[t], far[t]), jnp.where(x == 0, far[t], near[t])]
        full = jnp.concatenate(blocks, axis=1)
        for bit, pairs in zip(highs, swap_high, strict=True):
            other = send(full, pairs)
            full = jnp.concatenate(
                [jnp.where(bit == 0, full, other), jnp.where(bit == 0, other, full)], axis=1
            )
        return full

    def rows_full(near, far, place):
        x, highs = place[1], place[4]
        _, w, cols = near.shape
        full = in_order(x, near, far, 1).reshape(1, 2 * m * w, cols)
        for bit, pairs in zip(highs, swap_high, strict=True):
            full = in_order(bit, full, send(full, pairs), 0).reshape(1, -1, cols)
        return full.reshape(n * w, cols)

    def act_weights(down_full, cols, cols_act, w_act):
        w = 2 * w_act
        flat_act = high * w_act

        def rows_act(start):
            part = down_full[start : start + flat_act]
            return jnp.concatenate([widened(part[:, d * w : (d + 1) * w]) for d in range(n)])

        wide_act = (rows_act(cols), rows_act(cols + flat_act))
        last = down_full[cols + 2 * flat_act :]
        narrow_act = jnp.concatenate(
            [
                jnp.concatenate([last[:, d * w : d * w + w_act], last[:, d * w + w_act : (d + 1) * w]])
                for d in range(n)
            ],
            axis=1,
        )
        return wide_act, narrow_act

    def split_bit(array, bit, axis):
        mine = lax.dynamic_index_in_dim(array, bit, axis, keepdims=False)
        return mine, lax.dynamic_index_in_dim(array, 1 - bit, axis, keepdims=False)

    def split_columns(total, place):
        x, highs = place[1], place[4]
        w = total.shape[1] // n
        for bit, pairs in zip(reversed(highs), reversed(swap_high), strict=True):
            half = total.shape[1] // 2
            theirs = jnp.where(bit == 0, total[:, half:], total[:, :half])
            mine = jnp.where(bit == 0, total[:, :half], total[:, half:])
            total = add_low(mine, send(theirs, pairs))
        blocks = [total[:, d * w : (d + 1) * w] for d in range(2 * m)]
        theirs = [jnp.where(x == 0, blocks[2 * t + 1], blocks[2 * t]) for t in range(m)]
        mine = [jnp.where(x == 0, blocks[2 * t], blocks[2 * t + 1]) for t in range(m)]
        return jnp.stack(mine), jnp.stack(theirs)

    def split_rows(total, place):
        x, highs = place[1], place[4]
        w = total.shape[0] // n
        total = total.reshape(n, w, total.shape[1])
        for bit, pairs in zip(reversed(highs), reversed(swap_high), strict=True):
            mine, theirs = split_bit(total.reshape((2, -1) + total.shape[1:]), bit, 0)
            total = add_low(mine, send(theirs, pairs))
        return split_bit(total.reshape(m, 2, w, total.shape[2]), x, 1)

    def light_core(part, place):
        rows = part.shape[0] // (n * q)
        return split_bit(part.reshape(high * m, 2, 2, 2, rows, part.shape[1]), place[3], 3)

    def light_highs(part, place):
        highs = place[4]
        for bit, pairs in zip(reversed(highs), reversed(swap_high), strict=True):
            mine, theirs = split_bit(part.reshape((2, -1) + part.shape[1:]), bit, 0)
            part = add_low(mine, send(theirs, pairs))
        return part

    def add_all(pieces):
        total = pieces[0].astype(F32)
        for k in range(1, m):
            total = total + pieces[k].astype(F32)
        return total

    def pairs_of(mine, other):
        return jnp.concatenate([mine, other]).reshape(-1, mine.shape[-1])

    def core_order(rows):
        old, new = jnp.arange(HD)[:, None], jnp.arange(HD)[None, :]
        half = HD // 2
        same = (old // (2 * rows) == (new % half) // rows) & (old // rows % 2 == new // half)
        return (same & (old % rows == new % rows)).astype(BF16)

    def core_parts(blocks):
        half = blocks.shape[-1] // 2
        return [blocks[..., at : at + half].reshape(blocks.shape[0], -1) for at in (0, half)]

    def by_core(c, mine, other):
        width = mine.shape[-1]
        return [
            jnp.where(c == 0, mine, other).reshape(-1, width),
            jnp.where(c == 0, other, mine).reshape(-1, width),
        ]

    def narrowed(array):
        size = array.shape[-1] // high
        return jnp.concatenate([array[..., i * size : (i + 1) * size] for i in range(high)], axis=-2)

    def widened(array):
        size = array.shape[-2] // high
        return jnp.concatenate([array[..., i * size : (i + 1) * size, :] for i in range(high)], axis=-1)

    def cut(array, index, size, axis):
        return lax.dynamic_slice_in_dim(array, index * size, size, axis)

    def ffn_unit(gate_value, rows, up_weight, narrow):
        up_value = mm(rows, up_weight)
        hidden = gated_unit(gate_value, up_value).astype(BF16)
        return gate_value, up_value, hidden, mm(hidden, narrow).astype(BF16)

    def ffn_back(d_hidden, gate_value, up_value, wide):
        _, pullback = jax.vjp(gated_unit, gate_value, up_value)
        d_gate, d_up = pullback(d_hidden)
        d_gate, d_up = d_gate.astype(BF16), d_up.astype(BF16)
        d_rows = (mm_tr(d_gate, wide[0]) + mm_tr(d_up, wide[1])).astype(BF16)
        return d_rows, d_gate, d_up

    def per_device(
        prefix_tokens,
        actions,
        robot_state,
        text_len,
        flow_index,
        query_pre,
        key_pre,
        value_pre,
        out_pre,
        gain_attn_pre,
        gain_ffn_pre,
        query_act,
        key_act,
        value_act,
        out_act,
        gain_attn_act,
        gain_ffn_act,
        action_in,
        mix_first,
        mix_second,
        state_in,
        gate_pre,
        up_pre,
        down_pre,
        gate_act,
        up_act,
        down_act,
        grad_pre,
        grad_act,
    ):
        dp = lax.axis_index("dp")
        ctx = lax.axis_index("ctx")
        z, x = (dp // 2) % m, dp % 2
        y, c = ctx // 2, ctx % 2
        highs = [(dp // (2 * m * 2**i)) % 2 for i in range(len(swap_high))]
        place = (z, x, y, c, highs)
        width = prefix_tokens.shape[2]
        tokens = prefix_tokens.shape[1]
        rows_pre = -(-tokens // 32) * 32
        suffix = grad_act.shape[2]
        rows_act = -(-suffix // 32) * 32
        acts = actions.shape[2]
        devices = n * q
        r64, r32 = query_pre.shape[0], query_act.shape[0]

        cols = gate_pre.shape[1] // m
        cols_act = gate_act.shape[1] // m
        w = gate_pre.shape[0]
        w_act = gate_act.shape[0]
        flat_act = high * w_act
        half = width // 2 + HD
        at = width + 2 * HD
        scale = HD ** (-0.5)

        pad = jnp.zeros((r64 - r32,), BF16)
        gains = jnp.stack(
            [
                gain_attn_pre,
                gain_ffn_pre,
                jnp.concatenate([gain_attn_act, pad]),
                jnp.concatenate([gain_ffn_act, pad]),
            ],
            axis=1,
        )
        gains = jnp.pad(gains, ((0, 0), (0, 124)))
        first = jnp.concatenate([query_pre, key_pre, value_pre, gains], axis=1)
        small = jnp.pad(jnp.concatenate([action_in, state_in], axis=1), ((0, 0), (0, 64)))
        third = jnp.concatenate(
            [query_act, key_act, value_act, mix_second, small], axis=1
        )
        second = jnp.concatenate([out_pre, out_act, mix_first], axis=1)
        third_half = third.shape[1] // 256 * 128
        sharing = [
            [flat((h * m + a) * 2 + b, d) for a in range(m) for d in range(q)]
            for h in range(high)
            for b in range(2)
        ]

        def gather_act(block):
            return lax.all_gather(block, AXES, axis=0, tiled=True, axis_index_groups=sharing)

        def scatter_act(block):
            return lax.psum_scatter(
                block, AXES, scatter_dimension=0, tiled=True, axis_index_groups=sharing
            ).astype(F32)

        prefix_in = pad_rows(prefix_tokens[0], rows_pre).astype(F32)
        cot_own = pad_rows(grad_pre[0], rows_pre)
        piece_of = down_piece(down_pre, gate_act, up_act, down_act)
        down_own = jnp.stack([piece_of(t) for t in range(m)])
        gate_own = jnp.stack([gate_pre[:, t * cols : (t + 1) * cols] for t in range(m)])
        up_own = jnp.stack([up_pre[:, t * cols : (t + 1) * cols] for t in range(m)])

        first_z = z_gather(first)
        first_z, second = sync(first_z, second)
        first_z = with_highs(first_z, place)
        one_a, one_b = first_z[:, :, :half], first_z[:, :, half:]
        got_a, got_b = send(one_a, swap_y), send(one_b, swap_x)
        second_z = z_gather(second)
        got_a, got_b, third, cot_act_own = sync(got_a, got_b, third, pad_rows(grad_act[0, 0], rows_act))
        cot_all_act = gather_act(cot_act_own)
        one_a, one_b = in_order(y, one_a, got_a, 1), in_order(x, one_b, got_b, 1)
        got_a, got_b = send(one_a, swap_x), send(one_b, swap_y)
        got_a, got_b, third, second_z = sync(got_a, got_b, third, second_z)
        one_a, one_b = in_order(x, one_a, got_a, 1), in_order(y, one_b, got_b, 2)
        got_a, got_b = send(one_a, swap_c), send(one_b, swap_c)
        third_z = z_gather(third)
        second_z = with_highs(second_z, place)
        two_a, two_b = second_z[:, :, :width], second_z[:, :, width:]
        side_a, side_b = send(two_a, swap_y), send(two_b, swap_x)
        got_a, got_b, down_own = sync(got_a, got_b, down_own)
        first_a = in_order(c, one_a, got_a, 3).reshape(-1, half)
        first_b = in_order(c, one_b, got_b, 3).reshape(-1, half + 128)
        first_b, gain_cols = first_b[:, :half], first_b[:, half:]
        gain_rows = gain_cols.astype(F32)
        norm_attn, norm_ffn = gain_rows[:, 0], gain_rows[:, 1]
        gain_small = gain_rows[:, 2:4].reshape(devices, r64, 2)[:, :r32].reshape(devices * r32, 2)
        norm_attn_act, norm_ffn_act = gain_small[:, 0], gain_small[:, 1]
        normed_pre = rms_norm(prefix_in, norm_attn).astype(BF16)
        qkv_pre = jnp.concatenate(
            [mm(normed_pre, first_a).astype(BF16), mm(normed_pre, first_b).astype(BF16)], axis=1
        )
        ordered = core_order(r64)
        kv_own = jnp.concatenate(
            [qkv_pre[:, width : width + HD], mm(qkv_pre[:, width + HD :], ordered).astype(BF16)], axis=1
        )
        kv_own, side_a, side_b, third_z, down_own = sync(kv_own, side_a, side_b, third_z, down_own)
        down_z = z_swap(down_own)
        two_a, two_b = in_order(y, two_a, side_a, 1), in_order(x, two_b, side_b, 1)
        side_a, side_b = send(two_a, swap_x), send(two_b, swap_y)
        kv_y = send(kv_own, swap_y)
        kv_c = send(jnp.stack([kv_own, kv_y]), swap_c)
        (kv_c,) = sync(kv_c)
        queries_pre = qkv_pre[:, :width].reshape(rows_pre, HEADS, HD)
        both_kv = jnp.concatenate([kv_own[None], kv_y[None], kv_c]).reshape(q * rows_pre, 2 * HD)
        keys, values = both_kv[:, :HD], both_kv[:, HD:]
        key_count = q * rows_pre
        order = jnp.array([0, 2, 1, 3])
        spot = jnp.arange(rows_pre)
        positions = (ctx ^ order)[:, None] * tokens + spot[None, :]
        camera_rows = CAMS * PATCH
        key_valid = (positions < camera_rows) | (positions - camera_rows < text_len[0])
        key_valid = (key_valid & (spot < tokens)[None, :]).reshape(-1)

        def prefix_scores():
            scores = ein("qhd,kd->hqk", queries_pre, keys) * scale
            return jnp.where(key_valid[None, None, :], scores, masked_score)

        def soft_rows(scores):
            highest = jnp.max(scores, axis=-1, keepdims=True)
            totals = jnp.sum(jnp.exp(scores - highest), axis=-1, keepdims=True)
            log_total = highest + jnp.log(totals)
            return jnp.exp(scores - log_total), log_total

        probs_pre, total_pre = soft_rows(prefix_scores())
        probs_pre = probs_pre.astype(BF16)
        probs_pre, side_a, side_b, cot_all_act = sync(probs_pre, side_a, side_b, cot_all_act)
        two_a, two_b = in_order(x, two_a, side_a, 1), in_order(y, two_b, side_b, 2)
        side_a, side_b = send(two_a, swap_c), send(two_b, swap_c)
        attn_pre = ein("hqk,kd->qhd", probs_pre, values)
        attn_pre = attn_pre.astype(BF16)
        attn_pre, side_a, side_b, down_z, gate_own = sync(attn_pre, side_a, side_b, down_z, gate_own)
        gate_z = z_swap(gate_own)
        two = m // 2
        down_z_a, down_z_b = down_z[:two], down_z[two:]
        down_far_a = send(down_z_a, swap_x)
        out_parts = by_core(c, two_a, side_a)
        others = by_core(c, two_b, side_b)
        out_act_parts = [part[:, :DS] for part in others]
        mixer_parts = [part[:, DS:] for part in others]
        attn_parts = core_parts(attn_pre)
        mid_pre = prefix_in + mm(attn_parts[0], out_parts[0]) + mm(attn_parts[1], out_parts[1])
        normed_two_pre = rms_norm(mid_pre, norm_ffn).astype(BF16)
        normed_two_pre, cot_own, third_z, gate_z, up_own, down_far_a, down_z_b = sync(
            normed_two_pre, cot_own, third_z, gate_z, up_own, down_far_a, down_z_b
        )
        up_z = z_swap(up_own)
        down_far_b = send(down_z_b, swap_x)
        gate_far = send(gate_z, swap_x)
        third_z = with_highs(third_z, place)
        three_a, three_b = third_z[:, :, :third_half], third_z[:, :, third_half:]
        third_a, third_b = send(three_a, swap_y), send(three_b, swap_x)
        up_z, down_far_b, third_a, third_b = sync(up_z, down_far_b, third_a, third_b)
        row_z = z_gather(normed_two_pre)
        three_a, three_b = in_order(y, three_a, third_a, 1), in_order(x, three_b, third_b, 1)
        third_a, third_b = send(three_a, swap_x), send(three_b, swap_y)
        down_full = columns_full(down_z, jnp.concatenate([down_far_a, down_far_b]), place)
        third_a, third_b, gate_far, up_z = sync(third_a, third_b, gate_far, up_z)
        up_far = send(up_z, swap_x)
        gate_full = rows_full(gate_z, gate_far, place)
        three_a, three_b = in_order(x, three_a, third_a, 1), in_order(y, three_b, third_b, 2)
        third_a, third_b = send(three_a, swap_c), send(three_b, swap_c)
        third = jnp.concatenate(
            [
                in_order(c, three_a, third_a, 3).reshape(devices * r32, -1),
                in_order(c, three_b, third_b, 3).reshape(devices * r32, -1),
            ],
            axis=1,
        )
        qkv_act_w = third[:, :at]
        mixer_second = third[:, at : at + DS]
        action_full = third[:, at + DS : at + DS + 32]
        state_full = third[:, at + DS + 32 : at + DS + 64]
        time_rows = time_embed(flow_index[0, 0])
        action_emb = mm_tr(actions[0, 0], action_full)
        mix_input = jnp.concatenate(
            [action_emb, jnp.broadcast_to(time_rows[None, :], action_emb.shape)], axis=-1
        ).astype(BF16)
        mix_parts = core_parts(ein("tbk,kj->tbj", mix_input.reshape(acts, -1, HD), ordered).astype(BF16))
        pre_mix = mm(mix_parts[0], mixer_parts[0]) + mm(mix_parts[1], mixer_parts[1])
        mixed_act = jax.nn.silu(pre_mix).astype(BF16)
        action_rows = mm(mixed_act, mixer_second)
        state_row = mm_tr(robot_state, state_full)
        side_input = pad_rows(jnp.concatenate([state_row, action_rows], axis=0), rows_act)
        normed_act = rms_norm(side_input, norm_attn_act).astype(BF16)
        qkv_act = mm(normed_act, qkv_act_w).astype(BF16)
        row_z, qkv_act, gate_full, cot_own, down_full = sync(
            row_z, qkv_act, gate_full, cot_own, down_full
        )
        cot_z = z_gather(cot_own)
        row_got = send(row_z[:two], swap_y)
        narrow = down_full[:cols]
        wide_act, narrow_act = act_weights(down_full, cols, cols_act, w_act)
        queries_act = qkv_act[:, :width].reshape(rows_act, HEADS, HD)
        keys_act = qkv_act[:, width : width + HD]
        values_act = mm(qkv_act[:, width + HD :], ordered).astype(BF16)
        groups = jnp.arange(rows_act) > 0
        own_block = (groups[None, :] <= groups[:, None]) & (jnp.arange(rows_act) < suffix)[None, :]

        def side_scores():
            far = ein("qhd,kd->hqk", queries_act, keys) * scale
            far = jnp.where(key_valid[None, None, :], far, masked_score)
            near = ein("qhd,kd->hqk", queries_act, keys_act) * scale
            near = jnp.where(own_block[None], near, masked_score)
            return jnp.concatenate([far, near], axis=-1)

        probs_act, total_act = soft_rows(side_scores())
        probs_act_low = probs_act.astype(BF16)
        attn_act = ein("hqk,kd->qhd", probs_act_low[..., :key_count], values) + ein(
            "hqk,kd->qhd", probs_act_low[..., key_count:], values_act
        )
        attn_act_parts = core_parts(attn_act.astype(BF16))
        mid_act = (
            side_input + mm(attn_act_parts[0], out_act_parts[0]) + mm(attn_act_parts[1], out_act_parts[1])
        )
        normed_two_act = rms_norm(mid_act, norm_ffn_act).astype(BF16)
        row_got, normed_two_act, row_z_odd = sync(row_got, normed_two_act, row_z[two:])
        rows_all_act = gather_act(normed_two_act)
        near = pairs_of(row_z[:two], row_got)
        row_far = send(near, swap_c)
        row_got = send(row_z_odd, swap_y)
        up_full = rows_full(up_z, up_far, place)
        row_far, up_full = sync(row_far, up_full)
        row_e = jnp.concatenate([near, row_far])
        wide = (gate_full, up_full)
        unit_e = ffn_unit(mm(row_e, gate_full), row_e, up_full, narrow)
        row_got, part_e, cot_z = sync(row_got, unit_e[3], cot_z)
        near = pairs_of(row_z[two:], row_got)
        row_far = send(near, swap_c)
        cot_got = send(cot_z[:two], swap_y)
        cot_other_got = send(cot_z[two:], swap_y)
        (row_far,) = sync(row_far)
        row_o = jnp.concatenate([near, row_far])
        four_rows = 2 * two * rows_pre
        even_got = send(part_e[four_rows:], swap_c)
        unit_o = ffn_unit(mm(row_o, gate_full), row_o, up_full, narrow)
        even_got, cot_got, part_o = sync(even_got, cot_got, unit_o[3])
        near_e = pairs_of(cot_z[:two], cot_got)
        far_e = send(near_e, swap_c)
        cot_got = cot_other_got
        two_rows = 2 * rows_pre
        out_even = add_low(part_e[:four_rows], even_got)
        odd_got = send(part_o[four_rows:], swap_c)
        gate_act_value, up_act_value, hidden_act, part_act = ffn_unit(
            mm(rows_all_act, wide_act[0]), rows_all_act, wide_act[1], narrow_act
        )
        d_rows_act, d_gate_act, d_up_act = ffn_back(
            mm_tr(cot_all_act, narrow_act), gate_act_value, up_act_value, wide_act
        )
        grad_down_act = outer_sum(hidden_act, cot_all_act).astype(BF16)
        half_act = cols_act // 2

        def blocks_act(total):
            return jnp.concatenate(
                [narrowed(total[d * w_act : (d + 1) * w_act]) for d in range(n)], axis=1
            )

        narrow_parts = jnp.concatenate(
            [
                blocks_act(outer_sum(rows_all_act, d_gate_act).astype(BF16)),
                blocks_act(outer_sum(rows_all_act, d_up_act).astype(BF16)),
                jnp.concatenate(
                    [
                        grad_down_act[at_row : at_row + half_act, d * w_act : (d + 1) * w_act]
                        for d in range(n)
                        for at_row in (0, half_act)
                    ],
                    axis=1,
                ),
            ],
            axis=0,
        )
        small_mine, small_theirs = split_columns(narrow_parts, place)
        far_e, cot_got, odd_got, d_rows_act, part_act, small_theirs = sync(
            far_e, cot_got, odd_got, d_rows_act, part_act, small_theirs
        )
        d_branch_act = scatter_act(d_rows_act)
        small_got = send(small_theirs, swap_x)
        cot_e = jnp.concatenate([near_e, far_e])
        near_o = pairs_of(cot_z[two:], cot_got)
        far_o = send(near_o, swap_c)
        even_got = send(out_even[two_rows:], swap_y)
        d_hidden_e = mm_tr(cot_e, narrow)
        far_o, d_hidden_e = sync(far_o, d_hidden_e)
        cot_o = jnp.concatenate([near_o, far_o])
        grad_down = outer_sums([unit_e[2], unit_o[2]], [cot_e, cot_o])
        down_mine, down_theirs = split_columns(grad_down, place)
        d_hidden_o = mm_tr(cot_o, narrow)
        even_got, down_theirs, d_hidden_o, part_act = sync(even_got, down_theirs, d_hidden_o, part_act)
        branch_act = scatter_act(part_act)
        out_even = add_low(out_even[:two_rows], even_got)
        out_odd = add_low(part_o[:four_rows], odd_got)
        odd_got = send(out_odd[two_rows:], swap_y)
        down_got = send(down_theirs, swap_x)
        back_o = ffn_back(d_hidden_o, unit_o[0], unit_o[1], wide)
        odd_got, back_o_rows, small_got, down_got = sync(odd_got, back_o[0], small_got, down_got)
        out_odd = add_low(out_odd[:two_rows], odd_got)
        out_z = z_swap(jnp.concatenate([out_even, out_odd]).reshape(m, rows_pre, width))
        odd_got = send(back_o_rows[four_rows:], swap_c)
        back_e = ffn_back(d_hidden_e, unit_e[0], unit_e[1], wide)
        odd_got, back_e_rows = sync(odd_got, back_e[0])
        d_odd = add_low(back_o_rows[:four_rows], odd_got)
        odd_got = send(d_odd[two_rows:], swap_y)
        even_got = send(back_e_rows[four_rows:], swap_c)
        down_both = [add_low(down_mine, down_got), add_low(small_mine, small_got)]
        down_sums = jnp.concatenate(down_both, axis=1)
        grad_gate = outer_sums([row_e, row_o], [back_e[1], back_o[1]])
        odd_got, even_got, grad_gate, down_sums = sync(odd_got, even_got, grad_gate, down_sums)
        down_z = z_swap(down_sums)
        d_odd = add_low(d_odd[:two_rows], odd_got)
        d_even = add_low(back_e_rows[:four_rows], even_got)
        even_got = send(d_even[two_rows:], swap_y)
        gate_mine, gate_theirs = split_rows(grad_gate, place)
        gate_got = send(gate_theirs, swap_x)
        grad_up = outer_sums([row_e, row_o], [back_e[2], back_o[2]])
        even_got, grad_up, d_branch_act, branch_act = sync(even_got, grad_up, d_branch_act, branch_act)
        d_even = add_low(d_even[:two_rows], even_got)
        d_z = z_swap(jnp.concatenate([d_even, d_odd]).reshape(m, rows_pre, width))
        up_mine, up_theirs = split_rows(grad_up, place)
        up_got = send(up_theirs, swap_x)
        d_mid_act, grad_norm_ffn_act = norm_back(mid_act, norm_ffn_act, d_branch_act)
        d_mid_act = d_mid_act + pad_rows(grad_act[0, 0], rows_act).astype(F32)
        d_mid_act_low = d_mid_act.astype(BF16)
        grads_out_act = [outer_sum(part, d_mid_act_low).astype(BF16) for part in attn_act_parts]

        def heads_of(d_mid, parts):
            halves = [mm_tr(d_mid, part).astype(BF16).reshape(-1, HEADS, HD // 2) for part in parts]
            return jnp.concatenate(halves, axis=-1)

        d_attn_act = heads_of(d_mid_act_low, out_act_parts)
        probs_act = jnp.exp(side_scores() - total_act)
        probs_act_low = probs_act.astype(BF16)
        d_probs_act = jnp.concatenate(
            [ein("qhd,kd->hqk", d_attn_act, values), ein("qhd,kd->hqk", d_attn_act, values_act)], axis=-1
        )
        d_scores_act = probs_act * (
            d_probs_act - jnp.sum(probs_act * d_probs_act, axis=-1, keepdims=True)
        )
        d_scores_act = d_scores_act.astype(BF16)
        far, near = d_scores_act[..., :key_count], d_scores_act[..., key_count:]
        d_query_act = ein("hqk,kd->qhd", far, keys) + ein("hqk,kd->qhd", near, keys_act)
        d_query_act = (d_query_act * scale).reshape(rows_act, width).astype(BF16)
        d_keys_act = (ein("hqk,qhd->kd", near, queries_act) * scale).astype(BF16)
        d_values_act = ein("hqk,qhd->kd", probs_act_low[..., key_count:], d_attn_act).astype(BF16)
        d_values_act = mm_tr(d_values_act, ordered).astype(BF16)
        d_qkv_act = jnp.concatenate([d_query_act, d_keys_act, d_values_act], axis=1)
        d_normed_act = mm_tr(d_qkv_act, qkv_act_w)
        grad_qkv_act = outer_sum(normed_act, d_qkv_act).astype(BF16)
        d_side, grad_norm_attn_act = norm_back(side_input, norm_attn_act, d_normed_act)
        d_side = d_side + d_mid_act
        grad_state_in = outer_sum(d_side[:1].astype(BF16), robot_state)
        d_action_rows = d_side[1 : 1 + acts].astype(BF16)
        grad_mix_second = outer_sum(mixed_act, d_action_rows).astype(BF16)
        d_mixed = mm_tr(d_action_rows, mixer_second)
        _, silu_back = jax.vjp(jax.nn.silu, pre_mix)
        d_pre_mix = silu_back(d_mixed)[0].astype(BF16)
        grads_mix_first = [outer_sum(part, d_pre_mix).astype(BF16) for part in mix_parts]
        d_emb = [
            mm_tr(d_pre_mix, part[: DS // 2]).astype(BF16).reshape(acts, -1, HD // 2) for part in mixer_parts
        ]
        d_action_emb = ein("tbj,kj->tbk", jnp.concatenate(d_emb, axis=-1), ordered)
        d_action_emb = d_action_emb.astype(BF16).reshape(acts, DS)
        grad_action_in = outer_sum(d_action_emb, actions[0, 0])
        grad_actions = mm(d_action_emb, action_full)
        small_grads = jnp.pad(
            jnp.concatenate([grad_action_in, grad_state_in], axis=1).astype(BF16), ((0, 0), (0, 64))
        )
        three = jnp.concatenate([grad_qkv_act, grad_mix_second, small_grads], axis=1)
        mine_a, theirs_a = light_core(three[:, :third_half], place)
        mine_b, theirs_b = light_core(three[:, third_half:], place)

        def of_core(bit, pair):
            part = jnp.where(bit == 0, pair[0], pair[1])
            return part.reshape(high * m, 2, 2, r64, part.shape[1])

        twos = [grads_out_act, grads_mix_first]
        theirs_twos = [of_core(1 - c, pair) for pair in twos]
        (d_z, theirs_a, theirs_b, gate_got), theirs_twos, *twos = together(
            [[d_z, theirs_a, theirs_b, gate_got], theirs_twos] + twos
        )
        gate_z = z_swap(add_low(gate_mine, gate_got))
        got_a, got_b = send(theirs_a, swap_c), send(theirs_b, swap_c)
        two_got = [send(theirs, swap_c) for theirs in theirs_twos]
        d_branch = add_all(d_z)
        d_mid_pre, grad_norm_ffn = norm_back(mid_pre, norm_ffn, d_branch)
        d_mid_pre = d_mid_pre + cot_own.astype(F32)
        d_mid_low = d_mid_pre.astype(BF16)
        grads_out_pre = [outer_sum(part, d_mid_low).astype(BF16) for part in attn_parts]
        d_attn_pre = heads_of(d_mid_low, out_parts)
        theirs_out = of_core(1 - c, grads_out_pre)
        small_z = down_z[:, cols:]
        (d_attn_pre, up_got, got_a, got_b, theirs_out), two_got, grads_out_pre, *twos = together(
            [[d_attn_pre, up_got, got_a, got_b, theirs_out], two_got, grads_out_pre] + twos
        )
        out_got = send(theirs_out, swap_c)
        halves = [
            split_bit(add_low(of_core(c, pair), got), y, 2) for pair, got in zip(twos, two_got, strict=True)
        ]
        two_got = [send(part[1], swap_y) for part in halves]
        share_a, share_b = add_low(mine_a, got_a), add_low(mine_b, got_b)
        mine_a, theirs_a = split_bit(share_a, x, 1)
        mine_b, theirs_b = split_bit(share_b, y, 2)
        got_a, got_b = send(theirs_a, swap_x), send(theirs_b, swap_y)
        probs_pre = jnp.exp(prefix_scores() - total_pre)
        d_probs = ein("qhd,kd->hqk", d_attn_pre, values)
        d_probs, probs_pre, out_got, got_a, got_b = sync(d_probs, probs_pre, out_got, got_a, got_b)
        out_half = split_bit(add_low(of_core(c, grads_out_pre), out_got), x, 1)
        out_got = send(out_half[1], swap_x)
        d_scores = probs_pre * (d_probs - jnp.sum(probs_pre * d_probs, axis=-1, keepdims=True))
        d_scores = d_scores.astype(BF16)
        (d_scores,) = sync(d_scores)
        share_a, share_b = add_low(mine_a, got_a), add_low(mine_b, got_b)
        mine_a, theirs_a = split_bit(share_a, y, 1)
        mine_b, theirs_b = split_bit(share_b, x, 1)
        got_a, got_b = send(theirs_a, swap_y), send(theirs_b, swap_x)
        key_terms = ein("hqk,qhd->kd", d_scores, queries_pre) + ein("hqk,qhd->kd", far, queries_act)
        value_terms = ein("hqk,qhd->kd", probs_pre.astype(BF16), d_attn_pre)
        value_terms = value_terms + ein("hqk,qhd->kd", probs_act_low[..., :key_count], d_attn_act)
        kv_terms = jnp.concatenate([key_terms * scale, value_terms], axis=1).astype(BF16)
        kv_terms = kv_terms.reshape(q, rows_pre, 2 * HD)
        kv_got = send(kv_terms[2:], swap_c)
        d_query_pre = (ein("hqk,kd->qhd", d_scores, keys) * scale).reshape(rows_pre, width).astype(BF16)
        up_swapped = add_low(up_mine, up_got)
        (kv_got, d_query_pre, gate_z, up_swapped), two_got = together(
            [[kv_got, d_query_pre, gate_z, up_swapped], two_got]
        )
        up_z = z_swap(up_swapped)
        kv_pair = add_low(kv_terms[:2], kv_got)
        kv_got = send(kv_pair[1], swap_y)
        rest = width - half
        d_normed_pre = mm_tr(d_query_pre[:, :half], first_a)
        d_normed_pre = d_normed_pre + mm_tr(d_query_pre[:, half:], first_b[:, :rest])
        grad_query = outer_sum(normed_pre, d_query_pre).astype(BF16)
        halves = [
            split_bit(add_low(part[0], got), x, 1) for part, got in zip(halves, two_got, strict=True)
        ]
        two_got = [send(part[1], swap_x) for part in halves]
        kv_got, grad_query, out_got = sync(kv_got, grad_query, out_got)
        out_half = split_bit(add_low(out_half[0], out_got), y, 1)
        out_got = send(out_half[1], swap_y)
        d_kv = (kv_pair[0].astype(F32) + kv_got.astype(F32)).astype(BF16)
        d_kv = jnp.concatenate([d_kv[:, :HD], mm_tr(d_kv[:, HD:], ordered).astype(BF16)], axis=1)
        d_normed_pre = d_normed_pre + mm_tr(d_kv, first_b[:, rest:])
        grad_kv = outer_sum(normed_pre, d_kv).astype(BF16)
        grad_prefix, grad_norm_attn = norm_back(prefix_in, norm_attn, d_normed_pre)
        grad_prefix = (grad_prefix + d_mid_pre)[:tokens]
        act_gains = jnp.stack([grad_norm_attn_act, grad_norm_ffn_act], axis=1).reshape(devices, r32, 2)
        act_gains = jnp.pad(act_gains, ((0, 0), (0, r64 - r32), (0, 0))).reshape(devices * r64, 2)
        gain_grads = jnp.concatenate(
            [jnp.stack([grad_norm_attn, grad_norm_ffn], axis=1), act_gains], axis=1
        ).astype(BF16)
        gain_grads = jnp.pad(gain_grads, ((0, 0), (0, 124)))
        last_a, far_a = light_core(grad_query[:, :half], place)
        last_b, far_b = light_core(
            jnp.concatenate([grad_query[:, half:], grad_kv, gain_grads], axis=1), place
        )
        two_got, (got_a, got_b, far_a, far_b, out_got) = together(
            [two_got, [got_a, got_b, far_a, far_b, out_got]]
        )
        mine_twos = [add_low(out_half[0], out_got)]
        mine_twos += [add_low(part[0], got) for part, got in zip(halves, two_got, strict=True)]
        share_a, share_b = add_low(mine_a, got_a), add_low(mine_b, got_b)
        shares = jnp.concatenate([share_a, share_b], axis=2)
        wide_third = shares.shape[2] // 2
        shares = jnp.concatenate([shares[:, :, :wide_third], shares[:, :, wide_third:]], axis=1)
        second_sums = light_highs(jnp.concatenate(mine_twos + [shares], axis=2), place)
        last_got_a, last_got_b = send(far_a, swap_c), send(far_b, swap_c)
        last_got_a, last_got_b, second_sums, up_z = sync(last_got_a, last_got_b, second_sums, up_z)
        second_z = z_swap(second_sums)
        share_a, share_b = add_low(last_a, last_got_a), add_low(last_b, last_got_b)
        last_a, far_a = split_bit(share_a, x, 1)
        last_b, far_b = split_bit(share_b, y, 2)
        got_a, got_b = send(far_a, swap_x), send(far_b, swap_y)

        def beside(pieces):
            return jnp.concatenate([pieces[t] for t in range(m)], axis=1).astype(F32)

        grad_down_pre = down_z[:, :cols].reshape(m * cols, w).astype(F32)
        grad_gate_act = beside([widened(small_z[t, :flat_act]) for t in range(m)])
        grad_up_act = beside([widened(small_z[t, flat_act : 2 * flat_act]) for t in range(m)])
        last = small_z[:, 2 * flat_act :]
        grad_down_act = jnp.concatenate([last[:, :, :w_act], last[:, :, w_act:]], axis=1)
        grad_down_act = grad_down_act.reshape(m * cols_act, w_act).astype(F32)
        grad_gate_pre = beside(gate_z)
        out_prefix = (mid_pre + add_all(out_z))[:tokens]
        out_actions = (mid_act + branch_act)[:suffix]
        grad_up_pre = beside(up_z)
        got_a, got_b, grad_down_pre, grad_gate_pre, grad_up_pre, out_prefix, out_actions = sync(
            got_a, got_b, grad_down_pre, grad_gate_pre, grad_up_pre, out_prefix, out_actions
        )
        share_a, share_b = add_low(last_a, got_a), add_low(last_b, got_b)
        last_a, far_a = split_bit(share_a, y, 1)
        last_b, far_b = split_bit(share_b, x, 1)
        got_a, got_b = send(far_a, swap_y), send(far_b, swap_x)
        got_a, got_b, second_z = sync(got_a, got_b, second_z)
        got_second = add_all(second_z)
        got_third = got_second[:, width + 2 * DS :]
        got_third = jnp.concatenate([got_third[:r32], got_third[r32:]], axis=1)
        share_a, share_b = add_low(last_a, got_a), add_low(last_b, got_b)
        first_z = z_swap(light_highs(jnp.concatenate([share_a, share_b], axis=2), place))
        got_first = add_all(first_z)

        wide_end = width + 2 * HD
        tail = got_third[:, at + DS :]
        return (
            out_prefix[None],
            out_actions[None, None],
            grad_prefix[None],
            grad_actions[None, None],
            got_first[:, :width],
            got_first[:, width : width + HD],
            got_first[:, width + HD : wide_end],
            got_second[:, :width],
            got_first[:, wide_end],
            got_first[:, wide_end + 1],
            got_third[:, :width],
            got_third[:, width : width + HD],
            got_third[:, width + HD : wide_end],
            got_second[:, width : width + DS],
            got_first[:r32, wide_end + 2],
            got_first[:r32, wide_end + 3],
            tail[:, :32],
            got_second[:, width + DS : width + 2 * DS],
            got_third[:, at : at + DS],
            tail[:, 32:64],
            grad_gate_pre,
            grad_up_pre,
            grad_down_pre,
            grad_gate_act,
            grad_up_act,
            grad_down_act,
        )

    return per_device


def solution(mesh):
    rows = P(("dp", "ctx"), None)
    line = P(("dp", "ctx"))
    return jax.shard_map(
        make_body(mesh.shape["dp"], mesh.shape["ctx"]),
        mesh=mesh,
        in_specs=(
            P("dp", "ctx", None),
            P("dp", "ctx", None, None),
            P("dp", None),
            P("dp"),
            P("dp", "ctx"),
            rows,
            rows,
            rows,
            rows,
            line,
            line,
            rows,
            rows,
            rows,
            rows,
            line,
            line,
            rows,
            rows,
            rows,
            rows,
            P("dp", "ctx"),
            P("dp", "ctx"),
            P("ctx", "dp"),
            P("dp", "ctx"),
            P("dp", "ctx"),
            P("ctx", "dp"),
            P("dp", "ctx", None),
            P("dp", "ctx", None, None),
        ),
        out_specs=(
            P("dp", "ctx", None),
            P("dp", "ctx", None, None),
            P("dp", "ctx", None),
            P("dp", "ctx", None, None),
            rows,
            rows,
            rows,
            rows,
            line,
            line,
            rows,
            rows,
            rows,
            rows,
            line,
            line,
            rows,
            rows,
            rows,
            rows,
            P("dp", "ctx"),
            P("dp", "ctx"),
            P("ctx", "dp"),
            P("dp", "ctx"),
            P("dp", "ctx"),
            P("ctx", "dp"),
        ),
        check_vma=False,
    )
```

```python
import math

import jax
import jax.numpy as jnp
from jax import lax
from jax.experimental import pallas as pl
from jax.experimental.pallas import tpu as pltpu
from jax.sharding import PartitionSpec as P

DS = 1024
HEADS = 8
HD = 256
CAMS = 3
PATCH = 192
NTIME = 1000
AXES = ("dp", "ctx")

masked_score = -1e30
F32 = jnp.float32
BF16 = jnp.bfloat16


def rms_norm(values, norm_gain):
    return values * lax.rsqrt(jnp.mean(values * values, axis=-1, keepdims=True) + 1e-06) * norm_gain


def norm_back(values, norm_gain, cotangent):
    _, pullback = jax.vjp(rms_norm, values, norm_gain)
    return pullback(cotangent)


def time_embed(sample_index):
    flow_time = (sample_index.astype(F32) + 0.5) / NTIME
    halves = DS // 2
    fraction = jnp.arange(halves, dtype=F32) / (halves - 1)
    period = 0.004 * jnp.power(1000.0, fraction)
    angles = 2.0 * math.pi * flow_time[..., None] / period
    return jnp.concatenate([jnp.sin(angles), jnp.cos(angles)], axis=-1)


def mm(left, right):
    return jnp.dot(left, right, preferred_element_type=F32)


def mm_tr(left, right):
    return lax.dot_general(left, right, (((1,), (1,)), ((), ())), preferred_element_type=F32)


def outer_sum(left, right):
    return lax.dot_general(left, right, (((0,), (0,)), ((), ())), preferred_element_type=F32)


def ein(spec, left, right):
    return jnp.einsum(spec, left, right, preferred_element_type=F32)


def add_low(left, right):
    return (left.astype(F32) + right.astype(F32)).astype(BF16)


def sync(*arrays):
    return lax.optimization_barrier(arrays)


def together(groups):
    flat = sync(*[array for group in groups for array in group])
    out, at = [], 0
    for group in groups:
        out.append(list(flat[at : at + len(group)]))
        at += len(group)
    return out


def pad_rows(array, rows):
    return jnp.pad(array, ((0, rows - array.shape[0]), (0, 0)))


def gated_unit(gate_value, up_value):
    return jax.nn.gelu(gate_value, approximate=True) * up_value


VMEM_BYTES = 40 * 2**20


def outer_kernel(count, *refs):
    left, right, out_ref = refs[:count], refs[count : 2 * count], refs[2 * count]
    total = None
    for one, other in zip(left, right, strict=True):
        part = lax.dot_general(one[...], other[...], (((0,), (0,)), ((), ())), preferred_element_type=F32)
        total = part if total is None else total + part
    out_ref[...] = total.astype(BF16)


def outer_sums(lefts, rights, tile=256):
    count, rows = len(lefts), lefts[0].shape[0]
    height, width = lefts[0].shape[1], rights[0].shape[1]
    return pl.pallas_call(
        lambda *refs: outer_kernel(count, *refs),
        grid=(height // tile,),
        in_specs=[pl.BlockSpec((rows, tile), lambda i: (0, i))] * count
        + [pl.BlockSpec((rows, width), lambda i: (0, 0))] * count,
        out_specs=pl.BlockSpec((tile, width), lambda i: (i, 0)),
        out_shape=jax.ShapeDtypeStruct((height, width), BF16),
        compiler_params=pltpu.CompilerParams(vmem_limit_bytes=VMEM_BYTES),
        cost_estimate=pl.CostEstimate(
            flops=2 * count * rows * height * width,
            bytes_accessed=2 * count * rows * (height + width) + 2 * height * width,
            transcendentals=0,
        ),
    )(*lefts, *rights)


def make_body(n, q):
    m = 4 if n >= 8 else n // 2
    high = n // (2 * m)

    def flat(dp, ctx):
        return dp * q + ctx

    def xor_pairs(dp_mask, ctx_mask):
        return [(flat(d, c), flat(d ^ dp_mask, c ^ ctx_mask)) for d in range(n) for c in range(q)]

    swap_c = xor_pairs(0, 1)
    swap_y = xor_pairs(0, 2)
    swap_x = xor_pairs(1, 0)
    swap_high = [xor_pairs(2 * m * 2**i, 0) for i in range(high.bit_length() - 1)]

    lines_z = [
        [flat((h * m + z) * 2 + x, c) for z in range(m)] for h in range(high) for x in range(2) for c in range(q)
    ]

    def send(array, pairs):
        return lax.ppermute(array, AXES, pairs)

    def z_swap(parts):
        return lax.all_to_all(parts, AXES, 0, 0, axis_index_groups=lines_z)

    def z_gather(own):
        return z_swap(jnp.broadcast_to(own[None], (m,) + own.shape))

    def in_order(bit, mine, other, axis):
        return jnp.where(bit == 0, jnp.stack([mine, other], axis), jnp.stack([other, mine], axis))

    def with_highs(lines, place):
        lines = lines[None]
        for bit, pairs in zip(place[4], swap_high, strict=True):
            lines = in_order(bit, lines, send(lines, pairs), 0)
            lines = lines.reshape((-1,) + lines.shape[2:])
        return lines.reshape((-1,) + lines.shape[2:])

    def down_piece(down_pre, gate_act, up_act, down_act):
        cols = down_pre.shape[0] // m
        cols_act = gate_act.shape[1] // m

        def piece_of(t):
            last = cut(down_act, t, cols_act, 0)
            return jnp.concatenate(
                [
                    cut(down_pre, t, cols, 0),
                    narrowed(cut(gate_act, t, cols_act, 1)),
                    narrowed(cut(up_act, t, cols_act, 1)),
                    jnp.concatenate([last[: cols_act // 2], last[cols_act // 2 :]], axis=1),
                ],
                axis=0,
            )

        return piece_of

    def columns_full(near, far, place):
        x, highs = place[1], place[4]
        blocks = []
        for t in range(m):
            blocks += [jnp.where(x == 0, near[t], far[t]), jnp.where(x == 0, far[t], near[t])]
        full = jnp.concatenate(blocks, axis=1)
        for bit, pairs in zip(highs, swap_high, strict=True):
            other = send(full, pairs)
            full = jnp.concatenate(
                [jnp.where(bit == 0, full, other), jnp.where(bit == 0, other, full)], axis=1
            )
        return full

    def rows_full(near, far, place):
        x, highs = place[1], place[4]
        _, w, cols = near.shape
        full = in_order(x, near, far, 1).reshape(1, 2 * m * w, cols)
        for bit, pairs in zip(highs, swap_high, strict=True):
            full = in_order(bit, full, send(full, pairs), 0).reshape(1, -1, cols)
        return full.reshape(n * w, cols)

    def act_weights(down_full, cols, cols_act, w_act):
        w = 2 * w_act
        flat_act = high * w_act

        def rows_act(start):
            part = down_full[start : start + flat_act]
            return jnp.concatenate([widened(part[:, d * w : (d + 1) * w]) for d in range(n)])

        wide_act = (rows_act(cols), rows_act(cols + flat_act))
        last = down_full[cols + 2 * flat_act :]
        narrow_act = jnp.concatenate(
            [
                jnp.concatenate([last[:, d * w : d * w + w_act], last[:, d * w + w_act : (d + 1) * w]])
                for d in range(n)
            ],
            axis=1,
        )
        return wide_act, narrow_act

    def split_bit(array, bit, axis):
        mine = lax.dynamic_index_in_dim(array, bit, axis, keepdims=False)
        return mine, lax.dynamic_index_in_dim(array, 1 - bit, axis, keepdims=False)

    def split_columns(total, place):
        x, highs = place[1], place[4]
        w = total.shape[1] // n
        for bit, pairs in zip(reversed(highs), reversed(swap_high), strict=True):
            half = total.shape[1] // 2
            theirs = jnp.where(bit == 0, total[:, half:], total[:, :half])
            mine = jnp.where(bit == 0, total[:, :half], total[:, half:])
            total = add_low(mine, send(theirs, pairs))
        blocks = [total[:, d * w : (d + 1) * w] for d in range(2 * m)]
        theirs = [jnp.where(x == 0, blocks[2 * t + 1], blocks[2 * t]) for t in range(m)]
        mine = [jnp.where(x == 0, blocks[2 * t], blocks[2 * t + 1]) for t in range(m)]
        return jnp.stack(mine), jnp.stack(theirs)

    def split_rows(total, place):
        x, highs = place[1], place[4]
        w = total.shape[0] // n
        total = total.reshape(n, w, total.shape[1])
        for bit, pairs in zip(reversed(highs), reversed(swap_high), strict=True):
            mine, theirs = split_bit(total.reshape((2, -1) + total.shape[1:]), bit, 0)
            total = add_low(mine, send(theirs, pairs))
        return split_bit(total.reshape(m, 2, w, total.shape[2]), x, 1)

    def light_core(part, place):
        rows = part.shape[0] // (n * q)
        return split_bit(part.reshape(high * m, 2, 2, 2, rows, part.shape[1]), place[3], 3)

    def light_highs(part, place):
        highs = place[4]
        for bit, pairs in zip(reversed(highs), reversed(swap_high), strict=True):
            mine, theirs = split_bit(part.reshape((2, -1) + part.shape[1:]), bit, 0)
            part = add_low(mine, send(theirs, pairs))
        return part

    def add_all(pieces):
        total = pieces[0].astype(F32)
        for k in range(1, m):
            total = total + pieces[k].astype(F32)
        return total

    def pairs_of(mine, other):
        return jnp.concatenate([mine, other]).reshape(-1, mine.shape[-1])

    def core_order(rows):
        old, new = jnp.arange(HD)[:, None], jnp.arange(HD)[None, :]
        half = HD // 2
        same = (old // (2 * rows) == (new % half) // rows) & (old // rows % 2 == new // half)
        return (same & (old % rows == new % rows)).astype(BF16)

    def core_parts(blocks):
        half = blocks.shape[-1] // 2
        return [blocks[..., at : at + half].reshape(blocks.shape[0], -1) for at in (0, half)]

    def by_core(c, mine, other):
        width = mine.shape[-1]
        return [
            jnp.where(c == 0, mine, other).reshape(-1, width),
            jnp.where(c == 0, other, mine).reshape(-1, width),
        ]

    def narrowed(array):
        size = array.shape[-1] // high
        return jnp.concatenate([array[..., i * size : (i + 1) * size] for i in range(high)], axis=-2)

    def widened(array):
        size = array.shape[-2] // high
        return jnp.concatenate([array[..., i * size : (i + 1) * size, :] for i in range(high)], axis=-1)

    def cut(array, index, size, axis):
        return lax.dynamic_slice_in_dim(array, index * size, size, axis)

    def ffn_unit(gate_value, rows, up_weight, narrow):
        up_value = mm(rows, up_weight)
        hidden = gated_unit(gate_value, up_value).astype(BF16)
        return gate_value, up_value, hidden, mm(hidden, narrow).astype(BF16)

    def ffn_back(d_hidden, gate_value, up_value, wide):
        _, pullback = jax.vjp(gated_unit, gate_value, up_value)
        d_gate, d_up = pullback(d_hidden)
        d_gate, d_up = d_gate.astype(BF16), d_up.astype(BF16)
        d_rows = (mm_tr(d_gate, wide[0]) + mm_tr(d_up, wide[1])).astype(BF16)
        return d_rows, d_gate, d_up

    def per_device(
        prefix_tokens,
        actions,
        robot_state,
        text_len,
        flow_index,
        query_pre,
        key_pre,
        value_pre,
        out_pre,
        gain_attn_pre,
        gain_ffn_pre,
        query_act,
        key_act,
        value_act,
        out_act,
        gain_attn_act,
        gain_ffn_act,
        action_in,
        mix_first,
        mix_second,
        state_in,
        gate_pre,
        up_pre,
        down_pre,
        gate_act,
        up_act,
        down_act,
        grad_pre,
        grad_act,
    ):
        dp = lax.axis_index("dp")
        ctx = lax.axis_index("ctx")
        z, x = (dp // 2) % m, dp % 2
        y, c = ctx // 2, ctx % 2
        highs = [(dp // (2 * m * 2**i)) % 2 for i in range(len(swap_high))]
        place = (z, x, y, c, highs)
        width = prefix_tokens.shape[2]
        tokens = prefix_tokens.shape[1]
        rows_pre = -(-tokens // 32) * 32
        suffix = grad_act.shape[2]
        rows_act = -(-suffix // 32) * 32
        acts = actions.shape[2]
        devices = n * q
        r64, r32 = query_pre.shape[0], query_act.shape[0]

        cols = gate_pre.shape[1] // m
        cols_act = gate_act.shape[1] // m
        w = gate_pre.shape[0]
        w_act = gate_act.shape[0]
        flat_act = high * w_act
        half = width // 2 + HD
        at = width + 2 * HD
        scale = HD ** (-0.5)

        pad = jnp.zeros((r64 - r32,), BF16)
        gains = jnp.stack(
            [
                gain_attn_pre,
                gain_ffn_pre,
                jnp.concatenate([gain_attn_act, pad]),
                jnp.concatenate([gain_ffn_act, pad]),
            ],
            axis=1,
        )
        gains = jnp.pad(gains, ((0, 0), (0, 124)))
        first = jnp.concatenate([query_pre, key_pre, value_pre, gains], axis=1)
        small = jnp.pad(jnp.concatenate([action_in, state_in], axis=1), ((0, 0), (0, 64)))
        third = jnp.concatenate(
            [query_act, key_act, value_act, mix_second, small], axis=1
        )
        second = jnp.concatenate([out_pre, out_act, mix_first], axis=1)
        third_half = third.shape[1] // 256 * 128
        sharing = [
            [flat((h * m + a) * 2 + b, d) for a in range(m) for d in range(q)]
            for h in range(high)
            for b in range(2)
        ]

        def gather_act(block):
            return lax.all_gather(block, AXES, axis=0, tiled=True, axis_index_groups=sharing)

        prefix_in = pad_rows(prefix_tokens[0], rows_pre).astype(F32)
        cot_own = pad_rows(grad_pre[0], rows_pre)
        piece_of = down_piece(down_pre, gate_act, up_act, down_act)
        down_own = jnp.stack([piece_of(t) for t in range(m)])
        gate_own = jnp.stack([gate_pre[:, t * cols : (t + 1) * cols] for t in range(m)])
        up_own = jnp.stack([up_pre[:, t * cols : (t + 1) * cols] for t in range(m)])

        first_z = z_gather(first)
        first_z, second = sync(first_z, second)
        first_z = with_highs(first_z, place)
        one_a, one_b = first_z[:, :, :half], first_z[:, :, half:]
        got_a, got_b = send(one_a, swap_y), send(one_b, swap_x)
        second_z = z_gather(second)
        got_a, got_b, third, cot_act_own = sync(got_a, got_b, third, pad_rows(grad_act[0, 0], rows_act))
        cot_all_act = gather_act(cot_act_own)
        one_a, one_b = in_order(y, one_a, got_a, 1), in_order(x, one_b, got_b, 1)
        got_a, got_b = send(one_a, swap_x), send(one_b, swap_y)
        got_a, got_b, third, second_z = sync(got_a, got_b, third, second_z)
        one_a, one_b = in_order(x, one_a, got_a, 1), in_order(y, one_b, got_b, 2)
        got_a, got_b = send(one_a, swap_c), send(one_b, swap_c)
        third_z = z_gather(third)
        second_z = with_highs(second_z, place)
        two_a, two_b = second_z[:, :, :width], second_z[:, :, width:]
        side_a, side_b = send(two_a, swap_y), send(two_b, swap_x)
        got_a, got_b, down_own = sync(got_a, got_b, down_own)
        first_a = in_order(c, one_a, got_a, 3).reshape(-1, half)
        first_b = in_order(c, one_b, got_b, 3).reshape(-1, half + 128)
        first_b, gain_cols = first_b[:, :half], first_b[:, half:]
        gain_rows = gain_cols.astype(F32)
        norm_attn, norm_ffn = gain_rows[:, 0], gain_rows[:, 1]
        gain_small = gain_rows[:, 2:4].reshape(devices, r64, 2)[:, :r32].reshape(devices * r32, 2)
        norm_attn_act, norm_ffn_act = gain_small[:, 0], gain_small[:, 1]
        normed_pre = rms_norm(prefix_in, norm_attn).astype(BF16)
        qkv_pre = jnp.concatenate(
            [mm(normed_pre, first_a).astype(BF16), mm(normed_pre, first_b).astype(BF16)], axis=1
        )
        ordered = core_order(r64)
        kv_own = jnp.concatenate(
            [qkv_pre[:, width : width + HD], mm(qkv_pre[:, width + HD :], ordered).astype(BF16)], axis=1
        )
        kv_own, side_a, side_b, third_z, down_own = sync(kv_own, side_a, side_b, third_z, down_own)
        down_z = z_swap(down_own)
        two_a, two_b = in_order(y, two_a, side_a, 1), in_order(x, two_b, side_b, 1)
        side_a, side_b = send(two_a, swap_x), send(two_b, swap_y)
        kv_y = send(kv_own, swap_y)
        kv_c = send(jnp.stack([kv_own, kv_y]), swap_c)
        (kv_c,) = sync(kv_c)
        queries_pre = qkv_pre[:, :width].reshape(rows_pre, HEADS, HD)
        both_kv = jnp.concatenate([kv_own[None], kv_y[None], kv_c]).reshape(q * rows_pre, 2 * HD)
        keys, values = both_kv[:, :HD], both_kv[:, HD:]
        key_count = q * rows_pre
        order = jnp.array([0, 2, 1, 3])
        spot = jnp.arange(rows_pre)
        positions = (ctx ^ order)[:, None] * tokens + spot[None, :]
        camera_rows = CAMS * PATCH
        key_valid = (positions < camera_rows) | (positions - camera_rows < text_len[0])
        key_valid = (key_valid & (spot < tokens)[None, :]).reshape(-1)

        def prefix_scores():
            scores = ein("qhd,kd->hqk", queries_pre, keys) * scale
            return jnp.where(key_valid[None, None, :], scores, masked_score)

        def soft_rows(scores):
            highest = jnp.max(scores, axis=-1, keepdims=True)
            totals = jnp.sum(jnp.exp(scores - highest), axis=-1, keepdims=True)
            log_total = highest + jnp.log(totals)
            return jnp.exp(scores - log_total), log_total

        probs_pre, total_pre = soft_rows(prefix_scores())
        probs_pre = probs_pre.astype(BF16)
        probs_pre, side_a, side_b, cot_all_act = sync(probs_pre, side_a, side_b, cot_all_act)
        two_a, two_b = in_order(x, two_a, side_a, 1), in_order(y, two_b, side_b, 2)
        side_a, side_b = send(two_a, swap_c), send(two_b, swap_c)
        attn_pre = ein("hqk,kd->qhd", probs_pre, values)
        attn_pre = attn_pre.astype(BF16)
        attn_pre, side_a, side_b, down_z, gate_own = sync(attn_pre, side_a, side_b, down_z, gate_own)
        gate_z = z_swap(gate_own)
        two = m // 2
        down_z_a, down_z_b = down_z[:two], down_z[two:]
        down_far_a = send(down_z_a, swap_x)
        out_parts = by_core(c, two_a, side_a)
        others = by_core(c, two_b, side_b)
        out_act_parts = [part[:, :DS] for part in others]
        mixer_parts = [part[:, DS:] for part in others]
        attn_parts = core_parts(attn_pre)
        mid_pre = prefix_in + mm(attn_parts[0], out_parts[0]) + mm(attn_parts[1], out_parts[1])
        normed_two_pre = rms_norm(mid_pre, norm_ffn).astype(BF16)
        normed_two_pre, cot_own, third_z, down_far_a, down_z_b = sync(
            normed_two_pre, cot_own, third_z, down_far_a, down_z_b
        )
        down_far_b = send(down_z_b, swap_x)
        gate_z, up_own, down_far_b = sync(gate_z, up_own, down_far_b)
        up_z = z_swap(up_own)
        gate_far = send(gate_z, swap_x)
        third_z = with_highs(third_z, place)
        three_a, three_b = third_z[:, :, :third_half], third_z[:, :, third_half:]
        third_a, third_b = send(three_a, swap_y), send(three_b, swap_x)
        up_z, down_far_b, third_a, third_b = sync(up_z, down_far_b, third_a, third_b)
        row_z = z_gather(normed_two_pre)
        three_a, three_b = in_order(y, three_a, third_a, 1), in_order(x, three_b, third_b, 1)
        third_a, third_b = send(three_a, swap_x), send(three_b, swap_y)
        down_full = columns_full(down_z, jnp.concatenate([down_far_a, down_far_b]), place)
        gate_far, up_z = sync(gate_far, up_z)
        up_far = send(up_z, swap_x)
        gate_full = rows_full(gate_z, gate_far, place)
        third_a, third_b, gate_full = sync(third_a, third_b, gate_full)
        three_a, three_b = in_order(x, three_a, third_a, 1), in_order(y, three_b, third_b, 2)
        third_a, third_b = send(three_a, swap_c), send(three_b, swap_c)
        third = jnp.concatenate(
            [
                in_order(c, three_a, third_a, 3).reshape(devices * r32, -1),
                in_order(c, three_b, third_b, 3).reshape(devices * r32, -1),
            ],
            axis=1,
        )
        qkv_act_w = third[:, :at]
        mixer_second = third[:, at : at + DS]
        action_full = third[:, at + DS : at + DS + 32]
        state_full = third[:, at + DS + 32 : at + DS + 64]
        time_rows = time_embed(flow_index[0, 0])
        action_emb = mm_tr(actions[0, 0], action_full)
        mix_input = jnp.concatenate(
            [action_emb, jnp.broadcast_to(time_rows[None, :], action_emb.shape)], axis=-1
        ).astype(BF16)
        mix_parts = core_parts(ein("tbk,kj->tbj", mix_input.reshape(acts, -1, HD), ordered).astype(BF16))
        pre_mix = mm(mix_parts[0], mixer_parts[0]) + mm(mix_parts[1], mixer_parts[1])
        mixed_act = jax.nn.silu(pre_mix).astype(BF16)
        action_rows = mm(mixed_act, mixer_second)
        state_row = mm_tr(robot_state, state_full)
        side_input = pad_rows(jnp.concatenate([state_row, action_rows], axis=0), rows_act)
        normed_act = rms_norm(side_input, norm_attn_act).astype(BF16)
        qkv_act = mm(normed_act, qkv_act_w).astype(BF16)
        row_z, qkv_act, gate_full, cot_own, down_full = sync(
            row_z, qkv_act, gate_full, cot_own, down_full
        )
        cot_z = z_gather(cot_own)
        row_got = send(row_z[:two], swap_y)
        narrow = down_full[:cols]
        wide_act, narrow_act = act_weights(down_full, cols, cols_act, w_act)
        queries_act = qkv_act[:, :width].reshape(rows_act, HEADS, HD)
        keys_act = qkv_act[:, width : width + HD]
        values_act = mm(qkv_act[:, width + HD :], ordered).astype(BF16)
        groups = jnp.arange(rows_act) > 0
        own_block = (groups[None, :] <= groups[:, None]) & (jnp.arange(rows_act) < suffix)[None, :]

        def side_scores():
            far = ein("qhd,kd->hqk", queries_act, keys) * scale
            far = jnp.where(key_valid[None, None, :], far, masked_score)
            near = ein("qhd,kd->hqk", queries_act, keys_act) * scale
            near = jnp.where(own_block[None], near, masked_score)
            return jnp.concatenate([far, near], axis=-1)

        probs_act, total_act = soft_rows(side_scores())
        probs_act_low = probs_act.astype(BF16)
        attn_act = ein("hqk,kd->qhd", probs_act_low[..., :key_count], values) + ein(
            "hqk,kd->qhd", probs_act_low[..., key_count:], values_act
        )
        attn_act_parts = core_parts(attn_act.astype(BF16))
        mid_act = (
            side_input + mm(attn_act_parts[0], out_act_parts[0]) + mm(attn_act_parts[1], out_act_parts[1])
        )
        normed_two_act = rms_norm(mid_act, norm_ffn_act).astype(BF16)
        row_got, normed_two_act, row_z_odd, up_far = sync(row_got, normed_two_act, row_z[two:], up_far)
        rows_all_act = gather_act(normed_two_act)
        near = pairs_of(row_z[:two], row_got)
        row_far = send(near, swap_c)
        row_got = send(row_z_odd, swap_y)
        up_full = rows_full(up_z, up_far, place)
        row_far, up_full = sync(row_far, up_full)
        row_e = jnp.concatenate([near, row_far])
        wide = (gate_full, up_full)
        unit_e = ffn_unit(mm(row_e, gate_full), row_e, up_full, narrow)
        row_got, part_e, cot_z = sync(row_got, unit_e[3], cot_z)
        near = pairs_of(row_z[two:], row_got)
        row_far = send(near, swap_c)
        cot_got = send(cot_z[:two], swap_y)
        cot_other_got = send(cot_z[two:], swap_y)
        (row_far,) = sync(row_far)
        row_o = jnp.concatenate([near, row_far])
        four_rows = 2 * two * rows_pre
        even_got = send(part_e[four_rows:], swap_c)
        unit_o = ffn_unit(mm(row_o, gate_full), row_o, up_full, narrow)
        gate_act_value, up_act_value, hidden_act, part_act = ffn_unit(
            mm(rows_all_act, wide_act[0]), rows_all_act, wide_act[1], narrow_act
        )
        d_rows_act, d_gate_act, d_up_act = ffn_back(
            mm_tr(cot_all_act, narrow_act), gate_act_value, up_act_value, wide_act
        )
        grad_down_act = outer_sum(hidden_act, cot_all_act).astype(BF16)
        half_act = cols_act // 2

        def blocks_act(total):
            return jnp.concatenate(
                [narrowed(total[d * w_act : (d + 1) * w_act]) for d in range(n)], axis=1
            )

        narrow_parts = jnp.concatenate(
            [
                blocks_act(outer_sum(rows_all_act, d_gate_act).astype(BF16)),
                blocks_act(outer_sum(rows_all_act, d_up_act).astype(BF16)),
                jnp.concatenate(
                    [
                        grad_down_act[at_row : at_row + half_act, d * w_act : (d + 1) * w_act]
                        for d in range(n)
                        for at_row in (0, half_act)
                    ],
                    axis=1,
                ),
            ],
            axis=0,
        )
        small_mine, small_theirs = split_columns(narrow_parts, place)
        act_sums = jnp.concatenate(
            [part.reshape(m, 2, 2, rows_act, DS) for part in (part_act, d_rows_act)], axis=3
        )
        act_mine, act_theirs = split_bit(act_sums, c, 2)
        even_got, cot_got, part_o, act_theirs, small_theirs = sync(
            even_got, cot_got, unit_o[3], act_theirs, small_theirs
        )
        act_got = send(act_theirs, swap_c)
        small_got = send(small_theirs, swap_x)
        near_e = pairs_of(cot_z[:two], cot_got)
        far_e = send(near_e, swap_c)
        cot_got = cot_other_got
        two_rows = 2 * rows_pre
        out_even = add_low(part_e[:four_rows], even_got)
        even_got = send(out_even[two_rows:], swap_y)
        odd_got = send(part_o[four_rows:], swap_c)
        far_e, cot_got, odd_got, act_got = sync(far_e, cot_got, odd_got, act_got)
        act_mine, act_theirs = split_bit(add_low(act_mine, act_got), y, 1)
        act_got = send(act_theirs, swap_y)
        cot_e = jnp.concatenate([near_e, far_e])
        near_o = pairs_of(cot_z[two:], cot_got)
        far_o = send(near_o, swap_c)
        out_odd = add_low(part_o[:four_rows], odd_got)
        odd_got = send(out_odd[two_rows:], swap_y)
        d_hidden_e = mm_tr(cot_e, narrow)
        far_o, d_hidden_e, act_got, even_got = sync(far_o, d_hidden_e, act_got, even_got)
        act_mine = add_low(act_mine, act_got)
        act_z = z_swap(jnp.concatenate([act_mine[:, :rows_act], act_mine[:, rows_act:]], axis=2))
        cot_o = jnp.concatenate([near_o, far_o])
        grad_down = outer_sums([unit_e[2], unit_o[2]], [cot_e, cot_o])
        down_mine, down_theirs = split_columns(grad_down, place)
        d_hidden_o = mm_tr(cot_o, narrow)
        odd_got, down_theirs, d_hidden_o, act_z = sync(odd_got, down_theirs, d_hidden_o, act_z)
        out_even = add_low(out_even[:two_rows], even_got)
        out_odd = add_low(out_odd[:two_rows], odd_got)
        out_z = z_swap(jnp.concatenate([out_even, out_odd]).reshape(m, rows_pre, width))
        down_got = send(down_theirs, swap_x)
        back_o = ffn_back(d_hidden_o, unit_o[0], unit_o[1], wide)
        (back_o_rows,) = sync(back_o[0])
        odd_got = send(back_o_rows[four_rows:], swap_c)
        back_e = ffn_back(d_hidden_e, unit_e[0], unit_e[1], wide)
        odd_got, back_e_rows, row_e, row_o, small_got, down_got = sync(
            odd_got, back_e[0], row_e, row_o, small_got, down_got
        )
        d_odd = add_low(back_o_rows[:four_rows], odd_got)
        odd_got = send(d_odd[two_rows:], swap_y)
        even_got = send(back_e_rows[four_rows:], swap_c)
        down_both = [add_low(down_mine, down_got), add_low(small_mine, small_got)]
        down_z = z_swap(jnp.concatenate(down_both, axis=1))
        grad_gate = outer_sums([row_e, row_o], [back_e[1], back_o[1]])
        odd_got, even_got, grad_gate, row_e, row_o = sync(odd_got, even_got, grad_gate, row_e, row_o)
        d_odd = add_low(d_odd[:two_rows], odd_got)
        d_even = add_low(back_e_rows[:four_rows], even_got)
        even_got = send(d_even[two_rows:], swap_y)
        gate_mine, gate_theirs = split_rows(grad_gate, place)
        gate_got = send(gate_theirs, swap_x)
        grad_up = outer_sums([row_e, row_o], [back_e[2], back_o[2]])
        even_got, grad_up, act_z, gate_got = sync(even_got, grad_up, act_z, gate_got)
        d_even = add_low(d_even[:two_rows], even_got)
        d_z = z_swap(jnp.concatenate([d_even, d_odd]).reshape(m, rows_pre, width))
        up_mine, up_theirs = split_rows(grad_up, place)
        up_got = send(up_theirs, swap_x)
        act_total = add_all(act_z)
        branch_act, d_branch_act = act_total[:, :DS], act_total[:, DS:]
        d_mid_act, grad_norm_ffn_act = norm_back(mid_act, norm_ffn_act, d_branch_act)
        d_mid_act = d_mid_act + pad_rows(grad_act[0, 0], rows_act).astype(F32)
        d_mid_act_low = d_mid_act.astype(BF16)
        grads_out_act = [outer_sum(part, d_mid_act_low).astype(BF16) for part in attn_act_parts]

        def heads_of(d_mid, parts):
            halves = [mm_tr(d_mid, part).astype(BF16).reshape(-1, HEADS, HD // 2) for part in parts]
            return jnp.concatenate(halves, axis=-1)

        d_attn_act = heads_of(d_mid_act_low, out_act_parts)
        probs_act = jnp.exp(side_scores() - total_act)
        probs_act_low = probs_act.astype(BF16)
        d_probs_act = jnp.concatenate(
            [ein("qhd,kd->hqk", d_attn_act, values), ein("qhd,kd->hqk", d_attn_act, values_act)], axis=-1
        )
        d_scores_act = probs_act * (
            d_probs_act - jnp.sum(probs_act * d_probs_act, axis=-1, keepdims=True)
        )
        d_scores_act = d_scores_act.astype(BF16)
        far, near = d_scores_act[..., :key_count], d_scores_act[..., key_count:]
        d_query_act = ein("hqk,kd->qhd", far, keys) + ein("hqk,kd->qhd", near, keys_act)
        d_query_act = (d_query_act * scale).reshape(rows_act, width).astype(BF16)
        d_keys_act = (ein("hqk,qhd->kd", near, queries_act) * scale).astype(BF16)
        d_values_act = ein("hqk,qhd->kd", probs_act_low[..., key_count:], d_attn_act).astype(BF16)
        d_values_act = mm_tr(d_values_act, ordered).astype(BF16)
        d_qkv_act = jnp.concatenate([d_query_act, d_keys_act, d_values_act], axis=1)
        d_normed_act = mm_tr(d_qkv_act, qkv_act_w)
        grad_qkv_act = outer_sum(normed_act, d_qkv_act).astype(BF16)
        d_side, grad_norm_attn_act = norm_back(side_input, norm_attn_act, d_normed_act)
        d_side = d_side + d_mid_act
        grad_state_in = outer_sum(d_side[:1].astype(BF16), robot_state)
        d_action_rows = d_side[1 : 1 + acts].astype(BF16)
        grad_mix_second = outer_sum(mixed_act, d_action_rows).astype(BF16)
        d_mixed = mm_tr(d_action_rows, mixer_second)
        _, silu_back = jax.vjp(jax.nn.silu, pre_mix)
        d_pre_mix = silu_back(d_mixed)[0].astype(BF16)
        grads_mix_first = [outer_sum(part, d_pre_mix).astype(BF16) for part in mix_parts]
        d_emb = [
            mm_tr(d_pre_mix, part[: DS // 2]).astype(BF16).reshape(acts, -1, HD // 2) for part in mixer_parts
        ]
        d_action_emb = ein("tbj,kj->tbk", jnp.concatenate(d_emb, axis=-1), ordered)
        d_action_emb = d_action_emb.astype(BF16).reshape(acts, DS)
        grad_action_in = outer_sum(d_action_emb, actions[0, 0])
        grad_actions = mm(d_action_emb, action_full)
        small_grads = jnp.pad(
            jnp.concatenate([grad_action_in, grad_state_in], axis=1).astype(BF16), ((0, 0), (0, 64))
        )
        three = jnp.concatenate([grad_qkv_act, grad_mix_second, small_grads], axis=1)
        mine_a, theirs_a = light_core(three[:, :third_half], place)
        mine_b, theirs_b = light_core(three[:, third_half:], place)

        def of_core(bit, pair):
            part = jnp.where(bit == 0, pair[0], pair[1])
            return part.reshape(high * m, 2, 2, r64, part.shape[1])

        twos = [grads_out_act, grads_mix_first]
        theirs_twos = [of_core(1 - c, pair) for pair in twos]
        (d_z, theirs_a, theirs_b), theirs_twos, *twos = together(
            [[d_z, theirs_a, theirs_b], theirs_twos] + twos
        )
        gate_z = z_swap(add_low(gate_mine, gate_got))
        got_a, got_b = send(theirs_a, swap_c), send(theirs_b, swap_c)
        two_got = [send(theirs, swap_c) for theirs in theirs_twos]
        d_branch = add_all(d_z)
        d_mid_pre, grad_norm_ffn = norm_back(mid_pre, norm_ffn, d_branch)
        d_mid_pre = d_mid_pre + cot_own.astype(F32)
        d_mid_low = d_mid_pre.astype(BF16)
        grads_out_pre = [outer_sum(part, d_mid_low).astype(BF16) for part in attn_parts]
        d_attn_pre = heads_of(d_mid_low, out_parts)
        theirs_out = of_core(1 - c, grads_out_pre)
        small_z = down_z[:, cols:]
        (d_attn_pre, up_got, got_a, got_b, theirs_out), two_got, grads_out_pre, *twos = together(
            [[d_attn_pre, up_got, got_a, got_b, theirs_out], two_got, grads_out_pre] + twos
        )
        out_got = send(theirs_out, swap_c)
        halves = [
            split_bit(add_low(of_core(c, pair), got), y, 2) for pair, got in zip(twos, two_got, strict=True)
        ]
        two_got = [send(part[1], swap_y) for part in halves]
        share_a, share_b = add_low(mine_a, got_a), add_low(mine_b, got_b)
        mine_a, theirs_a = split_bit(share_a, x, 1)
        mine_b, theirs_b = split_bit(share_b, y, 2)
        got_a, got_b = send(theirs_a, swap_x), send(theirs_b, swap_y)
        probs_pre = jnp.exp(prefix_scores() - total_pre)
        d_probs = ein("qhd,kd->hqk", d_attn_pre, values)
        d_probs, probs_pre, out_got, got_a, got_b = sync(d_probs, probs_pre, out_got, got_a, got_b)
        out_half = split_bit(add_low(of_core(c, grads_out_pre), out_got), x, 1)
        out_got = send(out_half[1], swap_x)
        d_scores = probs_pre * (d_probs - jnp.sum(probs_pre * d_probs, axis=-1, keepdims=True))
        d_scores = d_scores.astype(BF16)
        (d_scores,) = sync(d_scores)
        share_a, share_b = add_low(mine_a, got_a), add_low(mine_b, got_b)
        mine_a, theirs_a = split_bit(share_a, y, 1)
        mine_b, theirs_b = split_bit(share_b, x, 1)
        got_a, got_b = send(theirs_a, swap_y), send(theirs_b, swap_x)
        key_terms = ein("hqk,qhd->kd", d_scores, queries_pre) + ein("hqk,qhd->kd", far, queries_act)
        value_terms = ein("hqk,qhd->kd", probs_pre.astype(BF16), d_attn_pre)
        value_terms = value_terms + ein("hqk,qhd->kd", probs_act_low[..., :key_count], d_attn_act)
        kv_terms = jnp.concatenate([key_terms * scale, value_terms], axis=1).astype(BF16)
        kv_terms = kv_terms.reshape(q, rows_pre, 2 * HD)
        kv_got = send(kv_terms[2:], swap_c)
        d_query_pre = (ein("hqk,kd->qhd", d_scores, keys) * scale).reshape(rows_pre, width).astype(BF16)
        up_swapped = add_low(up_mine, up_got)
        kv_got, d_query_pre, gate_z, up_swapped = sync(kv_got, d_query_pre, gate_z, up_swapped)
        up_z = z_swap(up_swapped)
        kv_pair = add_low(kv_terms[:2], kv_got)
        kv_got = send(kv_pair[1], swap_y)
        rest = width - half
        d_normed_pre = mm_tr(d_query_pre[:, :half], first_a)
        d_normed_pre = d_normed_pre + mm_tr(d_query_pre[:, half:], first_b[:, :rest])
        grad_query = outer_sum(normed_pre, d_query_pre).astype(BF16)
        (kv_got, grad_query, out_got), two_got = together([[kv_got, grad_query, out_got], two_got])
        halves = [
            split_bit(add_low(part[0], got), x, 1) for part, got in zip(halves, two_got, strict=True)
        ]
        two_got = [send(part[1], swap_x) for part in halves]
        out_half = split_bit(add_low(out_half[0], out_got), y, 1)
        out_got = send(out_half[1], swap_y)
        d_kv = (kv_pair[0].astype(F32) + kv_got.astype(F32)).astype(BF16)
        d_kv = jnp.concatenate([d_kv[:, :HD], mm_tr(d_kv[:, HD:], ordered).astype(BF16)], axis=1)
        d_normed_pre = d_normed_pre + mm_tr(d_kv, first_b[:, rest:])
        grad_kv = outer_sum(normed_pre, d_kv).astype(BF16)
        grad_prefix, grad_norm_attn = norm_back(prefix_in, norm_attn, d_normed_pre)
        grad_prefix = (grad_prefix + d_mid_pre)[:tokens]
        act_gains = jnp.stack([grad_norm_attn_act, grad_norm_ffn_act], axis=1).reshape(devices, r32, 2)
        act_gains = jnp.pad(act_gains, ((0, 0), (0, r64 - r32), (0, 0))).reshape(devices * r64, 2)
        gain_grads = jnp.concatenate(
            [jnp.stack([grad_norm_attn, grad_norm_ffn], axis=1), act_gains], axis=1
        ).astype(BF16)
        gain_grads = jnp.pad(gain_grads, ((0, 0), (0, 124)))
        last_a, far_a = light_core(grad_query[:, :half], place)
        last_b, far_b = light_core(
            jnp.concatenate([grad_query[:, half:], grad_kv, gain_grads], axis=1), place
        )
        two_got, (got_a, got_b, far_a, far_b, out_got) = together(
            [two_got, [got_a, got_b, far_a, far_b, out_got]]
        )
        mine_twos = [add_low(out_half[0], out_got)]
        mine_twos += [add_low(part[0], got) for part, got in zip(halves, two_got, strict=True)]
        share_a, share_b = add_low(mine_a, got_a), add_low(mine_b, got_b)
        shares = jnp.concatenate([share_a, share_b], axis=2)
        wide_third = shares.shape[2] // 2
        shares = jnp.concatenate([shares[:, :, :wide_third], shares[:, :, wide_third:]], axis=1)
        second_sums = light_highs(jnp.concatenate(mine_twos + [shares], axis=2), place)
        last_got_a, last_got_b = send(far_a, swap_c), send(far_b, swap_c)
        last_got_a, last_got_b, second_sums, up_z = sync(last_got_a, last_got_b, second_sums, up_z)
        second_z = z_swap(second_sums)
        share_a, share_b = add_low(last_a, last_got_a), add_low(last_b, last_got_b)
        last_a, far_a = split_bit(share_a, x, 1)
        last_b, far_b = split_bit(share_b, y, 2)
        got_a, got_b = send(far_a, swap_x), send(far_b, swap_y)

        def beside(pieces):
            return jnp.concatenate([pieces[t] for t in range(m)], axis=1).astype(F32)

        grad_down_pre = down_z[:, :cols].reshape(m * cols, w).astype(F32)
        grad_gate_act = beside([widened(small_z[t, :flat_act]) for t in range(m)])
        grad_up_act = beside([widened(small_z[t, flat_act : 2 * flat_act]) for t in range(m)])
        last = small_z[:, 2 * flat_act :]
        grad_down_act = jnp.concatenate([last[:, :, :w_act], last[:, :, w_act:]], axis=1)
        grad_down_act = grad_down_act.reshape(m * cols_act, w_act).astype(F32)
        grad_gate_pre = beside(gate_z)
        out_prefix = (mid_pre + add_all(out_z))[:tokens]
        out_actions = (mid_act + branch_act)[:suffix]
        grad_up_pre = beside(up_z)
        got_a, got_b, grad_down_pre, grad_gate_pre, grad_up_pre, out_prefix, out_actions = sync(
            got_a, got_b, grad_down_pre, grad_gate_pre, grad_up_pre, out_prefix, out_actions
        )
        share_a, share_b = add_low(last_a, got_a), add_low(last_b, got_b)
        last_a, far_a = split_bit(share_a, y, 1)
        last_b, far_b = split_bit(share_b, x, 1)
        got_a, got_b = send(far_a, swap_y), send(far_b, swap_x)
        got_a, got_b, second_z = sync(got_a, got_b, second_z)
        got_second = add_all(second_z)
        got_third = got_second[:, width + 2 * DS :]
        got_third = jnp.concatenate([got_third[:r32], got_third[r32:]], axis=1)
        share_a, share_b = add_low(last_a, got_a), add_low(last_b, got_b)
        first_z = z_swap(light_highs(jnp.concatenate([share_a, share_b], axis=2), place))
        got_first = add_all(first_z)

        wide_end = width + 2 * HD
        tail = got_third[:, at + DS :]
        return (
            out_prefix[None],
            out_actions[None, None],
            grad_prefix[None],
            grad_actions[None, None],
            got_first[:, :width],
            got_first[:, width : width + HD],
            got_first[:, width + HD : wide_end],
            got_second[:, :width],
            got_first[:, wide_end],
            got_first[:, wide_end + 1],
            got_third[:, :width],
            got_third[:, width : width + HD],
            got_third[:, width + HD : wide_end],
            got_second[:, width : width + DS],
            got_first[:r32, wide_end + 2],
            got_first[:r32, wide_end + 3],
            tail[:, :32],
            got_second[:, width + DS : width + 2 * DS],
            got_third[:, at : at + DS],
            tail[:, 32:64],
            grad_gate_pre,
            grad_up_pre,
            grad_down_pre,
            grad_gate_act,
            grad_up_act,
            grad_down_act,
        )

    return per_device


def solution(mesh):
    rows = P(("dp", "ctx"), None)
    line = P(("dp", "ctx"))
    return jax.shard_map(
        make_body(mesh.shape["dp"], mesh.shape["ctx"]),
        mesh=mesh,
        in_specs=(
            P("dp", "ctx", None),
            P("dp", "ctx", None, None),
            P("dp", None),
            P("dp"),
            P("dp", "ctx"),
            rows,
            rows,
            rows,
            rows,
            line,
            line,
            rows,
            rows,
            rows,
            rows,
            line,
            line,
            rows,
            rows,
            rows,
            rows,
            P("dp", "ctx"),
            P("dp", "ctx"),
            P("ctx", "dp"),
            P("dp", "ctx"),
            P("dp", "ctx"),
            P("ctx", "dp"),
            P("dp", "ctx", None),
            P("dp", "ctx", None, None),
        ),
        out_specs=(
            P("dp", "ctx", None),
            P("dp", "ctx", None, None),
            P("dp", "ctx", None),
            P("dp", "ctx", None, None),
            rows,
            rows,
            rows,
            rows,
            line,
            line,
            rows,
            rows,
            rows,
            rows,
            line,
            line,
            rows,
            rows,
            rows,
            rows,
            P("dp", "ctx"),
            P("dp", "ctx"),
            P("ctx", "dp"),
            P("dp", "ctx"),
            P("dp", "ctx"),
            P("ctx", "dp"),
        ),
        check_vma=False,
    )
```

```python
import math

import jax
import jax.numpy as jnp
from jax import lax
from jax.experimental import pallas as pl
from jax.experimental.pallas import tpu as pltpu
from jax.sharding import PartitionSpec as P

DS = 1024
HEADS = 8
HD = 256
CAMS = 3
PATCH = 192
NTIME = 1000
AXES = ("dp", "ctx")

masked_score = -1e30
F32 = jnp.float32
BF16 = jnp.bfloat16


def rms_norm(values, norm_gain):
    return values * lax.rsqrt(jnp.mean(values * values, axis=-1, keepdims=True) + 1e-06) * norm_gain


def norm_back(values, norm_gain, cotangent):
    _, pullback = jax.vjp(rms_norm, values, norm_gain)
    return pullback(cotangent)


def time_embed(sample_index):
    flow_time = (sample_index.astype(F32) + 0.5) / NTIME
    halves = DS // 2
    fraction = jnp.arange(halves, dtype=F32) / (halves - 1)
    period = 0.004 * jnp.power(1000.0, fraction)
    angles = 2.0 * math.pi * flow_time[..., None] / period
    return jnp.concatenate([jnp.sin(angles), jnp.cos(angles)], axis=-1)


def mm(left, right):
    return jnp.dot(left, right, preferred_element_type=F32)


def mm_tr(left, right):
    return lax.dot_general(left, right, (((1,), (1,)), ((), ())), preferred_element_type=F32)


def outer_sum(left, right):
    return lax.dot_general(left, right, (((0,), (0,)), ((), ())), preferred_element_type=F32)


def ein(spec, left, right):
    return jnp.einsum(spec, left, right, preferred_element_type=F32)


def add_low(left, right):
    return (left.astype(F32) + right.astype(F32)).astype(BF16)


def sync(*arrays):
    return lax.optimization_barrier(arrays)


def together(groups):
    flat = sync(*[array for group in groups for array in group])
    out, at = [], 0
    for group in groups:
        out.append(list(flat[at : at + len(group)]))
        at += len(group)
    return out


def pad_rows(array, rows):
    return jnp.pad(array, ((0, rows - array.shape[0]), (0, 0)))


def gated_unit(gate_value, up_value):
    return jax.nn.gelu(gate_value, approximate=True) * up_value


VMEM_BYTES = 40 * 2**20


def outer_kernel(count, *refs):
    left, right, out_ref = refs[:count], refs[count : 2 * count], refs[2 * count]
    total = None
    for one, other in zip(left, right, strict=True):
        part = lax.dot_general(one[...], other[...], (((0,), (0,)), ((), ())), preferred_element_type=F32)
        total = part if total is None else total + part
    out_ref[...] = total.astype(BF16)


def outer_sums(lefts, rights, tile=256):
    count, rows = len(lefts), lefts[0].shape[0]
    height, width = lefts[0].shape[1], rights[0].shape[1]
    return pl.pallas_call(
        lambda *refs: outer_kernel(count, *refs),
        grid=(height // tile,),
        in_specs=[pl.BlockSpec((rows, tile), lambda i: (0, i))] * count
        + [pl.BlockSpec((rows, width), lambda i: (0, 0))] * count,
        out_specs=pl.BlockSpec((tile, width), lambda i: (i, 0)),
        out_shape=jax.ShapeDtypeStruct((height, width), BF16),
        compiler_params=pltpu.CompilerParams(vmem_limit_bytes=VMEM_BYTES),
        cost_estimate=pl.CostEstimate(
            flops=2 * count * rows * height * width,
            bytes_accessed=2 * count * rows * (height + width) + 2 * height * width,
            transcendentals=0,
        ),
    )(*lefts, *rights)


def make_body(n, q):
    m = 4 if n >= 8 else n // 2
    high = n // (2 * m)

    def flat(dp, ctx):
        return dp * q + ctx

    def xor_pairs(dp_mask, ctx_mask):
        return [(flat(d, c), flat(d ^ dp_mask, c ^ ctx_mask)) for d in range(n) for c in range(q)]

    swap_c = xor_pairs(0, 1)
    swap_y = xor_pairs(0, 2)
    swap_x = xor_pairs(1, 0)
    swap_high = [xor_pairs(2 * m * 2**i, 0) for i in range(high.bit_length() - 1)]

    lines_z = [
        [flat((h * m + z) * 2 + x, c) for z in range(m)] for h in range(high) for x in range(2) for c in range(q)
    ]

    def send(array, pairs):
        return lax.ppermute(array, AXES, pairs)

    def z_swap(parts):
        return lax.all_to_all(parts, AXES, 0, 0, axis_index_groups=lines_z)

    def copies(own):
        return jnp.broadcast_to(own[None], (m,) + own.shape)

    def z_gather(own):
        return z_swap(copies(own))

    def in_order(bit, mine, other, axis):
        return jnp.where(bit == 0, jnp.stack([mine, other], axis), jnp.stack([other, mine], axis))

    def with_highs(lines, place):
        lines = lines[None]
        for bit, pairs in zip(place[4], swap_high, strict=True):
            lines = in_order(bit, lines, send(lines, pairs), 0)
            lines = lines.reshape((-1,) + lines.shape[2:])
        return lines.reshape((-1,) + lines.shape[2:])

    def down_piece(down_pre, gate_act, up_act, down_act):
        cols = down_pre.shape[0] // m
        cols_act = gate_act.shape[1] // m

        def piece_of(t):
            last = cut(down_act, t, cols_act, 0)
            return jnp.concatenate(
                [
                    cut(down_pre, t, cols, 0),
                    narrowed(cut(gate_act, t, cols_act, 1)),
                    narrowed(cut(up_act, t, cols_act, 1)),
                    jnp.concatenate([last[: cols_act // 2], last[cols_act // 2 :]], axis=1),
                ],
                axis=0,
            )

        return piece_of

    def columns_full(near, far, place):
        x, highs = place[1], place[4]
        blocks = []
        for t in range(m):
            blocks += [jnp.where(x == 0, near[t], far[t]), jnp.where(x == 0, far[t], near[t])]
        full = jnp.concatenate(blocks, axis=1)
        for bit, pairs in zip(highs, swap_high, strict=True):
            other = send(full, pairs)
            full = jnp.concatenate(
                [jnp.where(bit == 0, full, other), jnp.where(bit == 0, other, full)], axis=1
            )
        return full

    def rows_full(near, far, place):
        x, highs = place[1], place[4]
        _, w, cols = near.shape
        full = in_order(x, near, far, 1).reshape(1, 2 * m * w, cols)
        for bit, pairs in zip(highs, swap_high, strict=True):
            full = in_order(bit, full, send(full, pairs), 0).reshape(1, -1, cols)
        return full.reshape(n * w, cols)

    def act_weights(down_full, cols, cols_act, w_act):
        w = 2 * w_act
        flat_act = high * w_act

        def rows_act(start):
            part = down_full[start : start + flat_act]
            return jnp.concatenate([widened(part[:, d * w : (d + 1) * w]) for d in range(n)])

        wide_act = (rows_act(cols), rows_act(cols + flat_act))
        last = down_full[cols + 2 * flat_act :]
        narrow_act = jnp.concatenate(
            [
                jnp.concatenate([last[:, d * w : d * w + w_act], last[:, d * w + w_act : (d + 1) * w]])
                for d in range(n)
            ],
            axis=1,
        )
        return wide_act, narrow_act

    def split_bit(array, bit, axis):
        mine = lax.dynamic_index_in_dim(array, bit, axis, keepdims=False)
        return mine, lax.dynamic_index_in_dim(array, 1 - bit, axis, keepdims=False)

    def split_columns(total, place):
        x, highs = place[1], place[4]
        w = total.shape[1] // n
        for bit, pairs in zip(reversed(highs), reversed(swap_high), strict=True):
            half = total.shape[1] // 2
            theirs = jnp.where(bit == 0, total[:, half:], total[:, :half])
            mine = jnp.where(bit == 0, total[:, :half], total[:, half:])
            total = add_low(mine, send(theirs, pairs))
        blocks = [total[:, d * w : (d + 1) * w] for d in range(2 * m)]
        theirs = [jnp.where(x == 0, blocks[2 * t + 1], blocks[2 * t]) for t in range(m)]
        mine = [jnp.where(x == 0, blocks[2 * t], blocks[2 * t + 1]) for t in range(m)]
        return jnp.stack(mine), jnp.stack(theirs)

    def split_rows(total, place):
        x, highs = place[1], place[4]
        w = total.shape[0] // n
        total = total.reshape(n, w, total.shape[1])
        for bit, pairs in zip(reversed(highs), reversed(swap_high), strict=True):
            mine, theirs = split_bit(total.reshape((2, -1) + total.shape[1:]), bit, 0)
            total = add_low(mine, send(theirs, pairs))
        return split_bit(total.reshape(m, 2, w, total.shape[2]), x, 1)

    def light_core(part, place):
        rows = part.shape[0] // (n * q)
        return split_bit(part.reshape(high * m, 2, 2, 2, rows, part.shape[1]), place[3], 3)

    def light_highs(part, place):
        highs = place[4]
        for bit, pairs in zip(reversed(highs), reversed(swap_high), strict=True):
            mine, theirs = split_bit(part.reshape((2, -1) + part.shape[1:]), bit, 0)
            part = add_low(mine, send(theirs, pairs))
        return part

    def add_all(pieces):
        total = pieces[0].astype(F32)
        for k in range(1, m):
            total = total + pieces[k].astype(F32)
        return total

    def pairs_of(mine, other):
        return jnp.concatenate([mine, other]).reshape(-1, mine.shape[-1])

    def core_order(rows):
        old, new = jnp.arange(HD)[:, None], jnp.arange(HD)[None, :]
        half = HD // 2
        same = (old // (2 * rows) == (new % half) // rows) & (old // rows % 2 == new // half)
        return (same & (old % rows == new % rows)).astype(BF16)

    def core_parts(blocks):
        half = blocks.shape[-1] // 2
        return [blocks[..., at : at + half].reshape(blocks.shape[0], -1) for at in (0, half)]

    def by_core(c, mine, other):
        width = mine.shape[-1]
        return [
            jnp.where(c == 0, mine, other).reshape(-1, width),
            jnp.where(c == 0, other, mine).reshape(-1, width),
        ]

    def narrowed(array):
        size = array.shape[-1] // high
        return jnp.concatenate([array[..., i * size : (i + 1) * size] for i in range(high)], axis=-2)

    def widened(array):
        size = array.shape[-2] // high
        return jnp.concatenate([array[..., i * size : (i + 1) * size, :] for i in range(high)], axis=-1)

    def cut(array, index, size, axis):
        return lax.dynamic_slice_in_dim(array, index * size, size, axis)

    def ffn_unit(gate_value, rows, up_weight, narrow):
        up_value = mm(rows, up_weight)
        hidden = gated_unit(gate_value, up_value).astype(BF16)
        return gate_value, up_value, hidden, mm(hidden, narrow).astype(BF16)

    def ffn_back(d_hidden, gate_value, up_value, wide):
        _, pullback = jax.vjp(gated_unit, gate_value, up_value)
        d_gate, d_up = pullback(d_hidden)
        d_gate, d_up = d_gate.astype(BF16), d_up.astype(BF16)
        d_rows = (mm_tr(d_gate, wide[0]) + mm_tr(d_up, wide[1])).astype(BF16)
        return d_rows, d_gate, d_up

    def per_device(
        prefix_tokens,
        actions,
        robot_state,
        text_len,
        flow_index,
        query_pre,
        key_pre,
        value_pre,
        out_pre,
        gain_attn_pre,
        gain_ffn_pre,
        query_act,
        key_act,
        value_act,
        out_act,
        gain_attn_act,
        gain_ffn_act,
        action_in,
        mix_first,
        mix_second,
        state_in,
        gate_pre,
        up_pre,
        down_pre,
        gate_act,
        up_act,
        down_act,
        grad_pre,
        grad_act,
    ):
        dp = lax.axis_index("dp")
        ctx = lax.axis_index("ctx")
        z, x = (dp // 2) % m, dp % 2
        y, c = ctx // 2, ctx % 2
        highs = [(dp // (2 * m * 2**i)) % 2 for i in range(len(swap_high))]
        place = (z, x, y, c, highs)
        width = prefix_tokens.shape[2]
        tokens = prefix_tokens.shape[1]
        rows_pre = -(-tokens // 32) * 32
        suffix = grad_act.shape[2]
        rows_act = -(-suffix // 32) * 32
        acts = actions.shape[2]
        devices = n * q
        r64, r32 = query_pre.shape[0], query_act.shape[0]

        cols = gate_pre.shape[1] // m
        cols_act = gate_act.shape[1] // m
        w = gate_pre.shape[0]
        w_act = gate_act.shape[0]
        flat_act = high * w_act
        half = width // 2 + HD
        at = width + 2 * HD
        scale = HD ** (-0.5)

        pad = jnp.zeros((r64 - r32,), BF16)
        gains = jnp.stack(
            [
                gain_attn_pre,
                gain_ffn_pre,
                jnp.concatenate([gain_attn_act, pad]),
                jnp.concatenate([gain_ffn_act, pad]),
            ],
            axis=1,
        )
        gains = jnp.pad(gains, ((0, 0), (0, 124)))
        first = jnp.concatenate([query_pre, key_pre, value_pre, gains], axis=1)
        small = jnp.pad(jnp.concatenate([action_in, state_in], axis=1), ((0, 0), (0, 64)))
        third = jnp.concatenate(
            [query_act, key_act, value_act, mix_second, small], axis=1
        )
        second = jnp.concatenate([out_pre, out_act, mix_first], axis=1)
        third_half = third.shape[1] // 256 * 128
        sharing = [
            [flat((h * m + a) * 2 + b, d) for a in range(m) for d in range(q)]
            for h in range(high)
            for b in range(2)
        ]

        def gather_act(block):
            return lax.all_gather(block, AXES, axis=0, tiled=True, axis_index_groups=sharing)

        prefix_in = pad_rows(prefix_tokens[0], rows_pre).astype(F32)
        cot_own = pad_rows(grad_pre[0], rows_pre)
        piece_of = down_piece(down_pre, gate_act, up_act, down_act)
        down_own = jnp.stack([piece_of(t) for t in range(m)])
        gate_own = jnp.stack([gate_pre[:, t * cols : (t + 1) * cols] for t in range(m)])
        up_own = jnp.stack([up_pre[:, t * cols : (t + 1) * cols] for t in range(m)])

        first_z = z_gather(first)
        first_z, second_m = sync(first_z, copies(second))
        first_z = with_highs(first_z, place)
        one_a, one_b = first_z[:, :, :half], first_z[:, :, half:]
        got_a, got_b = send(one_a, swap_y), send(one_b, swap_x)
        second_z = z_swap(second_m)
        got_a, got_b, third_m, cot_act_own = sync(
            got_a, got_b, copies(third), pad_rows(grad_act[0, 0], rows_act)
        )
        cot_all_act = gather_act(cot_act_own)
        one_a, one_b = in_order(y, one_a, got_a, 1), in_order(x, one_b, got_b, 1)
        got_a, got_b = send(one_a, swap_x), send(one_b, swap_y)
        got_a, got_b, third_m, second_z = sync(got_a, got_b, third_m, second_z)
        one_a, one_b = in_order(x, one_a, got_a, 1), in_order(y, one_b, got_b, 2)
        got_a, got_b = send(one_a, swap_c), send(one_b, swap_c)
        third_z = z_swap(third_m)
        second_z = with_highs(second_z, place)
        two_a, two_b = second_z[:, :, :width], second_z[:, :, width:]
        side_a, side_b = send(two_a, swap_y), send(two_b, swap_x)
        got_a, got_b, down_own = sync(got_a, got_b, down_own)
        first_a = in_order(c, one_a, got_a, 3).reshape(-1, half)
        first_b = in_order(c, one_b, got_b, 3).reshape(-1, half + 128)
        first_b, gain_cols = first_b[:, :half], first_b[:, half:]
        gain_rows = gain_cols.astype(F32)
        norm_attn, norm_ffn = gain_rows[:, 0], gain_rows[:, 1]
        gain_small = gain_rows[:, 2:4].reshape(devices, r64, 2)[:, :r32].reshape(devices * r32, 2)
        norm_attn_act, norm_ffn_act = gain_small[:, 0], gain_small[:, 1]
        normed_pre = rms_norm(prefix_in, norm_attn).astype(BF16)
        qkv_pre = jnp.concatenate(
            [mm(normed_pre, first_a).astype(BF16), mm(normed_pre, first_b).astype(BF16)], axis=1
        )
        ordered = core_order(r64)
        kv_own = jnp.concatenate(
            [qkv_pre[:, width : width + HD], mm(qkv_pre[:, width + HD :], ordered).astype(BF16)], axis=1
        )
        kv_own, side_a, side_b, third_z, down_own = sync(kv_own, side_a, side_b, third_z, down_own)
        down_z = z_swap(down_own)
        two_a, two_b = in_order(y, two_a, side_a, 1), in_order(x, two_b, side_b, 1)
        kv_y, two_a, two_b = sync(send(kv_own, swap_y), two_a, two_b)
        side_a, side_b = send(two_a, swap_x), send(two_b, swap_y)
        kv_c = send(jnp.stack([kv_own, kv_y]), swap_c)
        (kv_c,) = sync(kv_c)
        queries_pre = qkv_pre[:, :width].reshape(rows_pre, HEADS, HD)
        both_kv = jnp.concatenate([kv_own[None], kv_y[None], kv_c]).reshape(q * rows_pre, 2 * HD)
        keys, values = both_kv[:, :HD], both_kv[:, HD:]
        key_count = q * rows_pre
        order = jnp.array([0, 2, 1, 3])
        spot = jnp.arange(rows_pre)
        positions = (ctx ^ order)[:, None] * tokens + spot[None, :]
        camera_rows = CAMS * PATCH
        key_valid = (positions < camera_rows) | (positions - camera_rows < text_len[0])
        key_valid = (key_valid & (spot < tokens)[None, :]).reshape(-1)

        def prefix_scores():
            scores = ein("qhd,kd->hqk", queries_pre, keys) * scale
            return jnp.where(key_valid[None, None, :], scores, masked_score)

        def soft_rows(scores):
            highest = jnp.max(scores, axis=-1, keepdims=True)
            totals = jnp.sum(jnp.exp(scores - highest), axis=-1, keepdims=True)
            log_total = highest + jnp.log(totals)
            return jnp.exp(scores - log_total), log_total

        probs_pre, total_pre = soft_rows(prefix_scores())
        probs_pre = probs_pre.astype(BF16)
        probs_pre, side_a, side_b, cot_all_act = sync(probs_pre, side_a, side_b, cot_all_act)
        two_a, two_b = in_order(x, two_a, side_a, 1), in_order(y, two_b, side_b, 2)
        side_a, side_b = send(two_a, swap_c), send(two_b, swap_c)
        attn_pre = ein("hqk,kd->qhd", probs_pre, values)
        attn_pre = attn_pre.astype(BF16)
        attn_pre, side_a, side_b, down_z, gate_own = sync(attn_pre, side_a, side_b, down_z, gate_own)
        gate_z = z_swap(gate_own)
        two = m // 2
        down_z_a, down_z_b = down_z[:two], down_z[two:]
        down_far_a = send(down_z_a, swap_x)
        out_parts = by_core(c, two_a, side_a)
        others = by_core(c, two_b, side_b)
        out_act_parts = [part[:, :DS] for part in others]
        mixer_parts = [part[:, DS:] for part in others]
        attn_parts = core_parts(attn_pre)
        mid_pre = prefix_in + mm(attn_parts[0], out_parts[0]) + mm(attn_parts[1], out_parts[1])
        normed_two_pre = rms_norm(mid_pre, norm_ffn).astype(BF16)
        normed_two_pre, cot_own, third_z, down_far_a, down_z_b = sync(
            normed_two_pre, cot_own, third_z, down_far_a, down_z_b
        )
        down_far_b = send(down_z_b, swap_x)
        gate_z, up_own = sync(gate_z, up_own)
        up_z = z_swap(up_own)
        down_far_b, gate_z = sync(down_far_b, gate_z)
        gate_far = send(gate_z, swap_x)
        third_z = with_highs(third_z, place)
        three_a, three_b = third_z[:, :, :third_half], third_z[:, :, third_half:]
        third_a, third_b = send(three_a, swap_y), send(three_b, swap_x)
        up_z, third_a, third_b = sync(up_z, third_a, third_b)
        row_z = z_gather(normed_two_pre)
        three_a, three_b = in_order(y, three_a, third_a, 1), in_order(x, three_b, third_b, 1)
        third_a, third_b = send(three_a, swap_x), send(three_b, swap_y)
        down_full = columns_full(down_z, jnp.concatenate([down_far_a, down_far_b]), place)
        gate_far, up_z = sync(gate_far, up_z)
        up_far = send(up_z, swap_x)
        gate_full = rows_full(gate_z, gate_far, place)
        third_a, third_b, gate_full = sync(third_a, third_b, gate_full)
        three_a, three_b = in_order(x, three_a, third_a, 1), in_order(y, three_b, third_b, 2)
        third_a, third_b = send(three_a, swap_c), send(three_b, swap_c)
        third = jnp.concatenate(
            [
                in_order(c, three_a, third_a, 3).reshape(devices * r32, -1),
                in_order(c, three_b, third_b, 3).reshape(devices * r32, -1),
            ],
            axis=1,
        )
        qkv_act_w = third[:, :at]
        mixer_second = third[:, at : at + DS]
        action_full = third[:, at + DS : at + DS + 32]
        state_full = third[:, at + DS + 32 : at + DS + 64]
        time_rows = time_embed(flow_index[0, 0])
        action_emb = mm_tr(actions[0, 0], action_full)
        mix_input = jnp.concatenate(
            [action_emb, jnp.broadcast_to(time_rows[None, :], action_emb.shape)], axis=-1
        ).astype(BF16)
        mix_parts = core_parts(ein("tbk,kj->tbj", mix_input.reshape(acts, -1, HD), ordered).astype(BF16))
        pre_mix = mm(mix_parts[0], mixer_parts[0]) + mm(mix_parts[1], mixer_parts[1])
        mixed_act = jax.nn.silu(pre_mix).astype(BF16)
        action_rows = mm(mixed_act, mixer_second)
        state_row = mm_tr(robot_state, state_full)
        side_input = pad_rows(jnp.concatenate([state_row, action_rows], axis=0), rows_act)
        normed_act = rms_norm(side_input, norm_attn_act).astype(BF16)
        qkv_act = mm(normed_act, qkv_act_w).astype(BF16)
        row_z, qkv_act, gate_full, cot_m, down_full = sync(
            row_z, qkv_act, gate_full, copies(cot_own), down_full
        )
        cot_z = z_swap(cot_m)
        row_got = send(row_z[:two], swap_y)
        narrow = down_full[:cols]
        wide_act, narrow_act = act_weights(down_full, cols, cols_act, w_act)
        queries_act = qkv_act[:, :width].reshape(rows_act, HEADS, HD)
        keys_act = qkv_act[:, width : width + HD]
        values_act = mm(qkv_act[:, width + HD :], ordered).astype(BF16)
        groups = jnp.arange(rows_act) > 0
        own_block = (groups[None, :] <= groups[:, None]) & (jnp.arange(rows_act) < suffix)[None, :]

        def side_scores():
            far = ein("qhd,kd->hqk", queries_act, keys) * scale
            far = jnp.where(key_valid[None, None, :], far, masked_score)
            near = ein("qhd,kd->hqk", queries_act, keys_act) * scale
            near = jnp.where(own_block[None], near, masked_score)
            return jnp.concatenate([far, near], axis=-1)

        probs_act, total_act = soft_rows(side_scores())
        probs_act_low = probs_act.astype(BF16)
        attn_act = ein("hqk,kd->qhd", probs_act_low[..., :key_count], values) + ein(
            "hqk,kd->qhd", probs_act_low[..., key_count:], values_act
        )
        attn_act_parts = core_parts(attn_act.astype(BF16))
        mid_act = (
            side_input + mm(attn_act_parts[0], out_act_parts[0]) + mm(attn_act_parts[1], out_act_parts[1])
        )
        normed_two_act = rms_norm(mid_act, norm_ffn_act).astype(BF16)
        row_got, normed_two_act, row_z_odd, up_far = sync(row_got, normed_two_act, row_z[two:], up_far)
        rows_all_act = gather_act(normed_two_act)
        near = pairs_of(row_z[:two], row_got)
        row_far = send(near, swap_c)
        row_got = send(row_z_odd, swap_y)
        up_full = rows_full(up_z, up_far, place)
        row_far, up_full = sync(row_far, up_full)
        row_e = jnp.concatenate([near, row_far])
        wide = (gate_full, up_full)
        unit_e = ffn_unit(mm(row_e, gate_full), row_e, up_full, narrow)
        row_got, part_e, cot_z = sync(row_got, unit_e[3], cot_z)
        near = pairs_of(row_z[two:], row_got)
        row_far = send(near, swap_c)
        cot_got = send(cot_z[:two], swap_y)
        cot_other_got = send(cot_z[two:], swap_y)
        (row_far,) = sync(row_far)
        row_o = jnp.concatenate([near, row_far])
        four_rows = 2 * two * rows_pre
        even_got = send(part_e[four_rows:], swap_c)
        unit_o = ffn_unit(mm(row_o, gate_full), row_o, up_full, narrow)
        gate_act_value, up_act_value, hidden_act, part_act = ffn_unit(
            mm(rows_all_act, wide_act[0]), rows_all_act, wide_act[1], narrow_act
        )
        d_rows_act, d_gate_act, d_up_act = ffn_back(
            mm_tr(cot_all_act, narrow_act), gate_act_value, up_act_value, wide_act
        )
        grad_down_act = outer_sum(hidden_act, cot_all_act).astype(BF16)
        half_act = cols_act // 2

        def blocks_act(total):
            return jnp.concatenate(
                [narrowed(total[d * w_act : (d + 1) * w_act]) for d in range(n)], axis=1
            )

        narrow_parts = jnp.concatenate(
            [
                blocks_act(outer_sum(rows_all_act, d_gate_act).astype(BF16)),
                blocks_act(outer_sum(rows_all_act, d_up_act).astype(BF16)),
                jnp.concatenate(
                    [
                        grad_down_act[at_row : at_row + half_act, d * w_act : (d + 1) * w_act]
                        for d in range(n)
                        for at_row in (0, half_act)
                    ],
                    axis=1,
                ),
            ],
            axis=0,
        )
        small_mine, small_theirs = split_columns(narrow_parts, place)
        act_sums = jnp.concatenate(
            [part.reshape(m, 2, 2, rows_act, DS) for part in (part_act, d_rows_act)], axis=3
        )
        act_mine, act_theirs = split_bit(act_sums, c, 2)
        even_got, cot_got, part_o, act_theirs, small_theirs = sync(
            even_got, cot_got, unit_o[3], act_theirs, small_theirs
        )
        act_got = send(act_theirs, swap_c)
        small_got = send(small_theirs, swap_x)
        near_e = pairs_of(cot_z[:two], cot_got)
        far_e = send(near_e, swap_c)
        cot_got = cot_other_got
        two_rows = 2 * rows_pre
        out_even = add_low(part_e[:four_rows], even_got)
        even_got = send(out_even[two_rows:], swap_y)
        odd_got = send(part_o[four_rows:], swap_c)
        far_e, cot_got, odd_got, act_got = sync(far_e, cot_got, odd_got, act_got)
        act_mine, act_theirs = split_bit(add_low(act_mine, act_got), y, 1)
        act_got = send(act_theirs, swap_y)
        cot_e = jnp.concatenate([near_e, far_e])
        near_o = pairs_of(cot_z[two:], cot_got)
        far_o = send(near_o, swap_c)
        out_odd = add_low(part_o[:four_rows], odd_got)
        odd_got = send(out_odd[two_rows:], swap_y)
        d_hidden_e = mm_tr(cot_e, narrow)
        far_o, d_hidden_e, even_got = sync(far_o, d_hidden_e, even_got)
        cot_o = jnp.concatenate([near_o, far_o])
        grad_down = outer_sums([unit_e[2], unit_o[2]], [cot_e, cot_o])
        down_mine, down_theirs = split_columns(grad_down, place)
        d_hidden_o = mm_tr(cot_o, narrow)
        odd_got, down_theirs, d_hidden_o = sync(odd_got, down_theirs, d_hidden_o)
        out_even = add_low(out_even[:two_rows], even_got)
        out_odd = add_low(out_odd[:two_rows], odd_got)
        out_z = z_swap(jnp.concatenate([out_even, out_odd]).reshape(m, rows_pre, width))
        down_got = send(down_theirs, swap_x)
        back_o = ffn_back(d_hidden_o, unit_o[0], unit_o[1], wide)
        (back_o_rows,) = sync(back_o[0])
        odd_got = send(back_o_rows[four_rows:], swap_c)
        back_e = ffn_back(d_hidden_e, unit_e[0], unit_e[1], wide)
        act_mine = add_low(act_mine, act_got)
        act_mine = jnp.concatenate([act_mine[:, :rows_act], act_mine[:, rows_act:]], axis=2)
        odd_got, back_e_rows, row_e, row_o, small_got, down_got, act_mine, out_z = sync(
            odd_got, back_e[0], row_e, row_o, small_got, down_got, act_mine, out_z
        )
        d_odd = add_low(back_o_rows[:four_rows], odd_got)
        odd_got = send(d_odd[two_rows:], swap_y)
        even_got = send(back_e_rows[four_rows:], swap_c)
        down_both = [add_low(down_mine, down_got), add_low(small_mine, small_got)]
        down_sums = jnp.concatenate(down_both, axis=1)
        act_z = z_swap(act_mine)
        grad_gate = outer_sums([row_e, row_o], [back_e[1], back_o[1]])
        odd_got, even_got, grad_gate, row_e, row_o, down_sums, act_z = sync(
            odd_got, even_got, grad_gate, row_e, row_o, down_sums, act_z
        )
        down_z = z_swap(down_sums)
        d_odd = add_low(d_odd[:two_rows], odd_got)
        d_even = add_low(back_e_rows[:four_rows], even_got)
        even_got = send(d_even[two_rows:], swap_y)
        gate_mine, gate_theirs = split_rows(grad_gate, place)
        gate_got = send(gate_theirs, swap_x)
        grad_up = outer_sums([row_e, row_o], [back_e[2], back_o[2]])
        even_got, grad_up, act_z, gate_got = sync(even_got, grad_up, act_z, gate_got)
        d_even = add_low(d_even[:two_rows], even_got)
        d_z = z_swap(jnp.concatenate([d_even, d_odd]).reshape(m, rows_pre, width))
        up_mine, up_theirs = split_rows(grad_up, place)
        up_got = send(up_theirs, swap_x)
        act_total = add_all(act_z)
        branch_act, d_branch_act = act_total[:, :DS], act_total[:, DS:]
        d_mid_act, grad_norm_ffn_act = norm_back(mid_act, norm_ffn_act, d_branch_act)
        d_mid_act = d_mid_act + pad_rows(grad_act[0, 0], rows_act).astype(F32)
        d_mid_act_low = d_mid_act.astype(BF16)
        grads_out_act = [outer_sum(part, d_mid_act_low).astype(BF16) for part in attn_act_parts]

        def heads_of(d_mid, parts):
            halves = [mm_tr(d_mid, part).astype(BF16).reshape(-1, HEADS, HD // 2) for part in parts]
            return jnp.concatenate(halves, axis=-1)

        d_attn_act = heads_of(d_mid_act_low, out_act_parts)
        probs_act = jnp.exp(side_scores() - total_act)
        probs_act_low = probs_act.astype(BF16)
        d_probs_act = jnp.concatenate(
            [ein("qhd,kd->hqk", d_attn_act, values), ein("qhd,kd->hqk", d_attn_act, values_act)], axis=-1
        )
        d_scores_act = probs_act * (
            d_probs_act - jnp.sum(probs_act * d_probs_act, axis=-1, keepdims=True)
        )
        d_scores_act = d_scores_act.astype(BF16)
        far, near = d_scores_act[..., :key_count], d_scores_act[..., key_count:]
        d_query_act = ein("hqk,kd->qhd", far, keys) + ein("hqk,kd->qhd", near, keys_act)
        d_query_act = (d_query_act * scale).reshape(rows_act, width).astype(BF16)
        d_keys_act = (ein("hqk,qhd->kd", near, queries_act) * scale).astype(BF16)
        d_values_act = ein("hqk,qhd->kd", probs_act_low[..., key_count:], d_attn_act).astype(BF16)
        d_values_act = mm_tr(d_values_act, ordered).astype(BF16)
        d_qkv_act = jnp.concatenate([d_query_act, d_keys_act, d_values_act], axis=1)
        d_normed_act = mm_tr(d_qkv_act, qkv_act_w)
        grad_qkv_act = outer_sum(normed_act, d_qkv_act).astype(BF16)
        d_side, grad_norm_attn_act = norm_back(side_input, norm_attn_act, d_normed_act)
        d_side = d_side + d_mid_act
        grad_state_in = outer_sum(d_side[:1].astype(BF16), robot_state)
        d_action_rows = d_side[1 : 1 + acts].astype(BF16)
        grad_mix_second = outer_sum(mixed_act, d_action_rows).astype(BF16)
        d_mixed = mm_tr(d_action_rows, mixer_second)
        _, silu_back = jax.vjp(jax.nn.silu, pre_mix)
        d_pre_mix = silu_back(d_mixed)[0].astype(BF16)
        grads_mix_first = [outer_sum(part, d_pre_mix).astype(BF16) for part in mix_parts]
        d_emb = [
            mm_tr(d_pre_mix, part[: DS // 2]).astype(BF16).reshape(acts, -1, HD // 2) for part in mixer_parts
        ]
        d_action_emb = ein("tbj,kj->tbk", jnp.concatenate(d_emb, axis=-1), ordered)
        d_action_emb = d_action_emb.astype(BF16).reshape(acts, DS)
        grad_action_in = outer_sum(d_action_emb, actions[0, 0])
        grad_actions = mm(d_action_emb, action_full)
        small_grads = jnp.pad(
            jnp.concatenate([grad_action_in, grad_state_in], axis=1).astype(BF16), ((0, 0), (0, 64))
        )
        three = jnp.concatenate([grad_qkv_act, grad_mix_second, small_grads], axis=1)
        mine_a, theirs_a = light_core(three[:, :third_half], place)
        mine_b, theirs_b = light_core(three[:, third_half:], place)

        def of_core(bit, pair):
            part = jnp.where(bit == 0, pair[0], pair[1])
            return part.reshape(high * m, 2, 2, r64, part.shape[1])

        twos = [grads_out_act, grads_mix_first]
        theirs_twos = [of_core(1 - c, pair) for pair in twos]
        (d_z, theirs_a, theirs_b, up_got), theirs_twos, *twos = together(
            [[d_z, theirs_a, theirs_b, up_got], theirs_twos] + twos
        )
        gate_z = z_swap(add_low(gate_mine, gate_got))
        got_a, got_b = send(theirs_a, swap_c), send(theirs_b, swap_c)
        two_got = [send(theirs, swap_c) for theirs in theirs_twos]
        d_branch = add_all(d_z)
        d_mid_pre, grad_norm_ffn = norm_back(mid_pre, norm_ffn, d_branch)
        d_mid_pre = d_mid_pre + cot_own.astype(F32)
        d_mid_low = d_mid_pre.astype(BF16)
        grads_out_pre = [outer_sum(part, d_mid_low).astype(BF16) for part in attn_parts]
        d_attn_pre = heads_of(d_mid_low, out_parts)
        theirs_out = of_core(1 - c, grads_out_pre)
        small_z = down_z[:, cols:]
        (d_attn_pre, got_a, got_b, theirs_out), two_got, grads_out_pre, *twos = together(
            [[d_attn_pre, got_a, got_b, theirs_out], two_got, grads_out_pre] + twos
        )
        out_got = send(theirs_out, swap_c)
        halves = [
            split_bit(add_low(of_core(c, pair), got), y, 2) for pair, got in zip(twos, two_got, strict=True)
        ]
        two_got = [send(part[1], swap_y) for part in halves]
        share_a, share_b = add_low(mine_a, got_a), add_low(mine_b, got_b)
        mine_a, theirs_a = split_bit(share_a, x, 1)
        mine_b, theirs_b = split_bit(share_b, y, 2)
        got_a, got_b = send(theirs_a, swap_x), send(theirs_b, swap_y)
        probs_pre = jnp.exp(prefix_scores() - total_pre)
        d_probs = ein("qhd,kd->hqk", d_attn_pre, values)
        d_probs, probs_pre, out_got = sync(d_probs, probs_pre, out_got)
        out_half = split_bit(add_low(of_core(c, grads_out_pre), out_got), x, 1)
        out_got = send(out_half[1], swap_x)
        d_scores = probs_pre * (d_probs - jnp.sum(probs_pre * d_probs, axis=-1, keepdims=True))
        d_scores = d_scores.astype(BF16)
        (d_scores,) = sync(d_scores)
        key_terms = ein("hqk,qhd->kd", d_scores, queries_pre) + ein("hqk,qhd->kd", far, queries_act)
        value_terms = ein("hqk,qhd->kd", probs_pre.astype(BF16), d_attn_pre)
        value_terms = value_terms + ein("hqk,qhd->kd", probs_act_low[..., :key_count], d_attn_act)
        kv_terms = jnp.concatenate([key_terms * scale, value_terms], axis=1).astype(BF16)
        kv_terms = kv_terms.reshape(q, rows_pre, 2 * HD)
        kv_got = send(kv_terms[2:], swap_c)
        d_query_pre = (ein("hqk,kd->qhd", d_scores, keys) * scale).reshape(rows_pre, width).astype(BF16)
        up_swapped = add_low(up_mine, up_got)
        kv_got, d_query_pre, gate_z, up_swapped, got_a, got_b = sync(
            kv_got, d_query_pre, gate_z, up_swapped, got_a, got_b
        )
        share_a, share_b = add_low(mine_a, got_a), add_low(mine_b, got_b)
        mine_a, theirs_a = split_bit(share_a, y, 1)
        mine_b, theirs_b = split_bit(share_b, x, 1)
        got_a, got_b = send(theirs_a, swap_y), send(theirs_b, swap_x)
        up_z = z_swap(up_swapped)
        kv_pair = add_low(kv_terms[:2], kv_got)
        kv_got = send(kv_pair[1], swap_y)
        rest = width - half
        d_normed_pre = mm_tr(d_query_pre[:, :half], first_a)
        d_normed_pre = d_normed_pre + mm_tr(d_query_pre[:, half:], first_b[:, :rest])
        grad_query = outer_sum(normed_pre, d_query_pre).astype(BF16)
        (kv_got, grad_query, out_got), two_got = together([[kv_got, grad_query, out_got], two_got])
        halves = [
            split_bit(add_low(part[0], got), x, 1) for part, got in zip(halves, two_got, strict=True)
        ]
        two_got = [send(part[1], swap_x) for part in halves]
        out_half = split_bit(add_low(out_half[0], out_got), y, 1)
        out_got = send(out_half[1], swap_y)
        d_kv = (kv_pair[0].astype(F32) + kv_got.astype(F32)).astype(BF16)
        d_kv = jnp.concatenate([d_kv[:, :HD], mm_tr(d_kv[:, HD:], ordered).astype(BF16)], axis=1)
        d_normed_pre = d_normed_pre + mm_tr(d_kv, first_b[:, rest:])
        grad_kv = outer_sum(normed_pre, d_kv).astype(BF16)
        grad_prefix, grad_norm_attn = norm_back(prefix_in, norm_attn, d_normed_pre)
        grad_prefix = (grad_prefix + d_mid_pre)[:tokens]
        act_gains = jnp.stack([grad_norm_attn_act, grad_norm_ffn_act], axis=1).reshape(devices, r32, 2)
        act_gains = jnp.pad(act_gains, ((0, 0), (0, r64 - r32), (0, 0))).reshape(devices * r64, 2)
        gain_grads = jnp.concatenate(
            [jnp.stack([grad_norm_attn, grad_norm_ffn], axis=1), act_gains], axis=1
        ).astype(BF16)
        gain_grads = jnp.pad(gain_grads, ((0, 0), (0, 124)))
        last_a, far_a = light_core(grad_query[:, :half], place)
        last_b, far_b = light_core(
            jnp.concatenate([grad_query[:, half:], grad_kv, gain_grads], axis=1), place
        )
        two_got, (got_a, got_b, far_a, far_b, out_got) = together(
            [two_got, [got_a, got_b, far_a, far_b, out_got]]
        )
        mine_twos = [add_low(out_half[0], out_got)]
        mine_twos += [add_low(part[0], got) for part, got in zip(halves, two_got, strict=True)]
        share_a, share_b = add_low(mine_a, got_a), add_low(mine_b, got_b)
        shares = jnp.concatenate([share_a, share_b], axis=2)
        wide_third = shares.shape[2] // 2
        shares = jnp.concatenate([shares[:, :, :wide_third], shares[:, :, wide_third:]], axis=1)
        second_sums = light_highs(jnp.concatenate(mine_twos + [shares], axis=2), place)
        last_got_a, last_got_b = send(far_a, swap_c), send(far_b, swap_c)
        last_got_a, last_got_b, second_sums, up_z = sync(last_got_a, last_got_b, second_sums, up_z)
        second_z = z_swap(second_sums)
        share_a, share_b = add_low(last_a, last_got_a), add_low(last_b, last_got_b)
        last_a, far_a = split_bit(share_a, x, 1)
        last_b, far_b = split_bit(share_b, y, 2)
        got_a, got_b = send(far_a, swap_x), send(far_b, swap_y)

        def beside(pieces):
            return jnp.concatenate([pieces[t] for t in range(m)], axis=1).astype(F32)

        grad_down_pre = down_z[:, :cols].reshape(m * cols, w).astype(F32)
        grad_gate_act = beside([widened(small_z[t, :flat_act]) for t in range(m)])
        grad_up_act = beside([widened(small_z[t, flat_act : 2 * flat_act]) for t in range(m)])
        last = small_z[:, 2 * flat_act :]
        grad_down_act = jnp.concatenate([last[:, :, :w_act], last[:, :, w_act:]], axis=1)
        grad_down_act = grad_down_act.reshape(m * cols_act, w_act).astype(F32)
        grad_gate_pre = beside(gate_z)
        out_prefix = (mid_pre + add_all(out_z))[:tokens]
        out_actions = (mid_act + branch_act)[:suffix]
        grad_up_pre = beside(up_z)
        got_a, got_b, grad_down_pre, grad_gate_pre, grad_up_pre, out_prefix, out_actions = sync(
            got_a, got_b, grad_down_pre, grad_gate_pre, grad_up_pre, out_prefix, out_actions
        )
        share_a, share_b = add_low(last_a, got_a), add_low(last_b, got_b)
        last_a, far_a = split_bit(share_a, y, 1)
        last_b, far_b = split_bit(share_b, x, 1)
        got_a, got_b = send(far_a, swap_y), send(far_b, swap_x)
        got_a, got_b, second_z = sync(got_a, got_b, second_z)
        got_second = add_all(second_z)
        got_third = got_second[:, width + 2 * DS :]
        got_third = jnp.concatenate([got_third[:r32], got_third[r32:]], axis=1)
        share_a, share_b = add_low(last_a, got_a), add_low(last_b, got_b)
        first_z = z_swap(light_highs(jnp.concatenate([share_a, share_b], axis=2), place))
        got_first = add_all(first_z)

        wide_end = width + 2 * HD
        tail = got_third[:, at + DS :]
        return (
            out_prefix[None],
            out_actions[None, None],
            grad_prefix[None],
            grad_actions[None, None],
            got_first[:, :width],
            got_first[:, width : width + HD],
            got_first[:, width + HD : wide_end],
            got_second[:, :width],
            got_first[:, wide_end],
            got_first[:, wide_end + 1],
            got_third[:, :width],
            got_third[:, width : width + HD],
            got_third[:, width + HD : wide_end],
            got_second[:, width : width + DS],
            got_first[:r32, wide_end + 2],
            got_first[:r32, wide_end + 3],
            tail[:, :32],
            got_second[:, width + DS : width + 2 * DS],
            got_third[:, at : at + DS],
            tail[:, 32:64],
            grad_gate_pre,
            grad_up_pre,
            grad_down_pre,
            grad_gate_act,
            grad_up_act,
            grad_down_act,
        )

    return per_device


def solution(mesh):
    rows = P(("dp", "ctx"), None)
    line = P(("dp", "ctx"))
    return jax.shard_map(
        make_body(mesh.shape["dp"], mesh.shape["ctx"]),
        mesh=mesh,
        in_specs=(
            P("dp", "ctx", None),
            P("dp", "ctx", None, None),
            P("dp", None),
            P("dp"),
            P("dp", "ctx"),
            rows,
            rows,
            rows,
            rows,
            line,
            line,
            rows,
            rows,
            rows,
            rows,
            line,
            line,
            rows,
            rows,
            rows,
            rows,
            P("dp", "ctx"),
            P("dp", "ctx"),
            P("ctx", "dp"),
            P("dp", "ctx"),
            P("dp", "ctx"),
            P("ctx", "dp"),
            P("dp", "ctx", None),
            P("dp", "ctx", None, None),
        ),
        out_specs=(
            P("dp", "ctx", None),
            P("dp", "ctx", None, None),
            P("dp", "ctx", None),
            P("dp", "ctx", None, None),
            rows,
            rows,
            rows,
            rows,
            line,
            line,
            rows,
            rows,
            rows,
            rows,
            line,
            line,
            rows,
            rows,
            rows,
            rows,
            P("dp", "ctx"),
            P("dp", "ctx"),
            P("ctx", "dp"),
            P("dp", "ctx"),
            P("dp", "ctx"),
            P("ctx", "dp"),
        ),
        check_vma=False,
    )
```
